512 devices in a mesh: lat: 16 (over z_lo, x, core), lon: 32 (over y, z_hi).
Axes of the slice: x: 4, y: 8, z: 8 (z_hi: 4, z_lo: 2; z = z_hi * 2 + z_lo), core: 2. Of those that a mesh axis runs over, the one named last changes fastest.
Arguments:
- tokens: bfloat16 [2, 96, 384, 192], P(None, 'lat', 'lon'), may hold values from -6 to 6
- gain_one: float32 [192], replicated, may hold values from 0.1 to 1.9
- gain_two: float32 [192], replicated, may hold values from 0.1 to 1.9
- qkv_weight: bfloat16 [192, 576], replicated, may hold values from -0.4375 to 0.4375
- proj_weight: bfloat16 [192, 192], replicated, may hold values from -0.4375 to 0.4375
- up_weight: bfloat16 [192, 768], replicated, may hold values from -0.4375 to 0.4375
- down_weight: bfloat16 [768, 192], replicated, may hold values from -0.21875 to 0.21875
- bias_table: float32 [6, 1, 16, 3312], P(None, None, 'lat'), may hold values from -6 to 306
- pos_index: int32 [144, 144], replicated, may hold values from 0 to 3311
- mask_ids: int32 [2, 96, 384], P(None, 'lat', 'lon'), may hold values from 0 to 2
- cotangent: bfloat16 [2, 96, 384, 192], P(None, 'lat', 'lon'), may hold values from -6 to 6
Outputs:
- output: bfloat16 [2, 96, 384, 192], P(None, 'lat', 'lon')
- delta_tokens: bfloat16 [2, 96, 384, 192], P(None, 'lat', 'lon')
- grad_gain_one: float32 [192], replicated
- grad_gain_two: float32 [192], replicated
- grad_qkv: float32 [192, 576], replicated
- grad_proj: float32 [192, 192], replicated
- grad_up: float32 [192, 768], replicated
- grad_down: float32 [768, 192], replicated
- grad_bias: float32 [6, 1, 16, 3312], P(None, None, 'lat')
The draws below stay inside these ranges and needn't reach their ends.
All inputs are finite; a program needn't handle non-finite values.
Results may differ from the reference program's by a relative error of at most 0.025.
Values may be sent and summed in bfloat16 or wider, within the bound.
No kernel may reach another device: no remote copies, remote signals or barrier semaphores. Data moves between devices by JAX's collectives and lax.ppermute only.
A program may use at most 64 MiB of HBM per device.

```python
import jax
import jax.numpy as jnp
from jax import lax

C = 192
HEADS = 6
HID = 768
WZ = 2
WLAT = 6
WLON = 12
WT = 144
NPOS = 3312
Z = 2
NLAT = 96
NLON = 384
NZW = 1
NLW = 16
TOKENS = 73728


def draw_bias_table(key, part):
    key = jax.random.fold_in(key, 11)
    first = jax.random.fold_in(key, 0)
    shape = (HEADS, NZW, NLW, NPOS)
    base = jnp.clip(jax.random.normal(first, shape, jnp.float32), -6.0, 6.0)
    return base


def set_ends(result, stream_key, least, high):
    shape = result.shape
    spot = [jax.random.randint(jax.random.fold_in(stream_key, axis), (), 0, shape[axis]) for axis in range(len(shape))]
    result = result.at[tuple(spot)].set(least)
    longest = shape.index(max(shape))
    spot[longest] = (spot[longest] + 1) % shape[longest]
    return result.at[tuple(spot)].set(high)


def steps_of(stream_key, shape, cuts, smallest, largest):
    def one(axis_at, blocks):
        heights = jax.random.uniform(jax.random.fold_in(jax.random.fold_in(stream_key, 6), axis_at), (blocks,), jnp.float32, smallest / len(cuts), largest / len(cuts))
        return jnp.repeat(jnp.exp(heights), shape[axis_at] // blocks).reshape((-1,) + (1,) * (len(shape) - axis_at - 1))

    level = one(*cuts[0])
    for cut in cuts[1:]:
        level = level * one(*cut)
    return level


def gaussian(key, extent, scale, reach, cuts=(), dtype=jnp.bfloat16):
    drawn = scale * jax.random.normal(key, extent, jnp.float32)
    if cuts:
        drawn = drawn * steps_of(key, extent, cuts, -0.22, 0.18)
    return jnp.clip(drawn, -reach, reach).astype(dtype)


def setup_inputs(seed: int = 0) -> dict:
    streams_of = jax.random.split(jax.random.key(seed), 12)
    tokens = gaussian(streams_of[0], (Z, NLAT, NLON, C), 1.0, 6.0, ((1, 16), (2, 32)))
    gain_one = jnp.clip(1.0 + 0.18 * jax.random.normal(streams_of[1], (C,), jnp.float32), 0.1, 1.9)
    gain_two = jnp.clip(1.0 + 0.18 * jax.random.normal(streams_of[2], (C,), jnp.float32), 0.1, 1.9)
    qkv_weight = gaussian(streams_of[3], (C, 3 * C), C ** -0.5, 0.4375)
    proj_weight = gaussian(streams_of[4], (C, C), C ** -0.5, 0.4375)
    up_weight = gaussian(streams_of[5], (C, HID), C ** -0.5, 0.4375)
    down_weight = gaussian(streams_of[6], (HID, C), HID ** -0.5, 0.21875)
    bias_table = draw_bias_table(jax.random.fold_in(streams_of[11], 71), 0)
    pos_index = set_ends(jax.random.randint(streams_of[8], (WT, WT), 0, NPOS), jax.random.fold_in(streams_of[8], 1), 0, NPOS - 1).astype(jnp.int32)
    mask_ids = set_ends(jax.random.randint(streams_of[9], (Z, NLAT, NLON), 0, 3), jax.random.fold_in(streams_of[9], 1), 0, 2).astype(jnp.int32)
    cotangent = gaussian(streams_of[10], (Z, NLAT, NLON, C), 1.0, 6.0, ((1, 16), (2, 32)))
    return {"tokens": tokens, "gain_one": gain_one, "gain_two": gain_two, "qkv_weight": qkv_weight, "proj_weight": proj_weight, "up_weight": up_weight, "down_weight": down_weight, "bias_table": bias_table, "pos_index": pos_index, "mask_ids": mask_ids, "cotangent": cotangent}


EPS = 1e-05

def norm_stats(values):
    widened = values.astype(jnp.float32)
    center = widened - lax.optimization_barrier(jnp.mean(widened, axis=-1, keepdims=True))
    spread = lax.optimization_barrier(jnp.mean(center * center, axis=-1, keepdims=True))
    inverse = lax.rsqrt(spread + EPS)
    return (center * inverse, inverse)

def norm_back(delta_hidden, normal, inverse, gain):
    grad_gain = lax.optimization_barrier(jnp.sum((delta_hidden * normal).reshape(-1, normal.shape[-1]), axis=0))
    delta_normal = delta_hidden * gain
    delta_input = inverse * (delta_normal - lax.optimization_barrier(jnp.mean(delta_normal, axis=-1, keepdims=True)) - normal * lax.optimization_barrier(jnp.mean(delta_normal * normal, axis=-1, keepdims=True)))
    return (delta_input, grad_gain)

def gelu_pair(up_proj):
    cumulative = 0.5 * (1.0 + lax.erf(up_proj * 0.7071067811865476))
    density = jnp.exp(-0.5 * up_proj * up_proj) * 0.3989422804014327
    return (up_proj * cumulative, cumulative + up_proj * density)

def mlp_block(middle, gain_two, up_weight, down_weight, cotangent):
    normal, inverse = norm_stats(middle)
    normed = (normal * gain_two).astype(jnp.bfloat16)
    up_proj = jnp.dot(normed, up_weight, preferred_element_type=jnp.float32)
    active, slope = gelu_pair(up_proj)
    active = active.astype(jnp.bfloat16)
    output = (middle.astype(jnp.float32) + jnp.dot(active, down_weight, preferred_element_type=jnp.float32)).astype(jnp.bfloat16)
    grad_down = jnp.dot(active.T, cotangent, preferred_element_type=jnp.float32)
    delta_act = jnp.dot(cotangent, down_weight.T, preferred_element_type=jnp.float32)
    delta_up = (delta_act * slope).astype(jnp.bfloat16)
    grad_up = jnp.dot(normed.T, delta_up, preferred_element_type=jnp.float32)
    delta_hidden = jnp.dot(delta_up, up_weight.T, preferred_element_type=jnp.float32)
    delta_input, grad_gain = norm_back(delta_hidden, normal, inverse, gain_two)
    delta_middle = (cotangent.astype(jnp.float32) + delta_input).astype(jnp.bfloat16)
    return (output, delta_middle, grad_gain, grad_up, grad_down)

def to_windows(layout):
    levels, lat_rows, lon_cols, features = layout.shape
    layout = layout.reshape(levels // WZ, WZ, lat_rows // WLAT, WLAT, lon_cols // WLON, WLON, features)
    layout = layout.transpose(2, 0, 4, 1, 3, 5, 6)
    return layout.reshape(lat_rows // WLAT, levels // WZ, lon_cols // WLON, WZ * WLAT * WLON, features)

def from_windows(windows, levels, lat_rows, lon_cols):
    features = windows.shape[-1]
    windows = windows.reshape(lat_rows // WLAT, levels // WZ, lon_cols // WLON, WZ, WLAT, WLON, features)
    windows = windows.transpose(1, 3, 0, 4, 2, 5, 6)
    return windows.reshape(levels, lat_rows, lon_cols, features)

def bias_pairs(bias_table, pos_index):
    head_count, level_blocks, lat_blocks = bias_table.shape[:3]
    picked = jnp.take(bias_table, pos_index.reshape(-1), axis=3)
    picked = picked.reshape(head_count, level_blocks, lat_blocks, WT, WT).transpose(2, 1, 0, 3, 4)
    return picked[:, :, None]

def table_grad(delta_type, pos_index):
    lat_blocks, level_blocks, head_count = delta_type.shape[:3]
    flattened = delta_type.reshape(lat_blocks, level_blocks, head_count, WT * WT).transpose(3, 2, 1, 0)
    summed = jax.ops.segment_sum(flattened, pos_index.reshape(-1), num_segments=NPOS)
    return summed.transpose(1, 2, 3, 0)

def attend(windows, mask_win, bias_win, qkv_weight):
    leading = windows.shape[:-2]
    features = windows.shape[-1]
    head_size = features // HEADS
    packed = jnp.dot(windows.reshape(-1, features), qkv_weight, preferred_element_type=jnp.float32)
    packed = lax.optimization_barrier(packed.astype(jnp.bfloat16))
    packed = packed.reshape(leading + (WT, 3, HEADS, head_size))
    queries = packed[..., 0, :, :]
    key_heads = packed[..., 1, :, :]
    values = packed[..., 2, :, :]
    factor = head_size ** (-0.5)
    scores = jnp.einsum('...phd,...rhd->...hpr', queries.astype(jnp.float32), key_heads.astype(jnp.float32)) * factor + bias_win
    allowed = mask_win[..., None, :, None] == mask_win[..., None, None, :]
    scores = jnp.where(allowed, scores, -1e+30)
    row_top = lax.optimization_barrier(jnp.max(scores, axis=-1, keepdims=True))
    weight = jnp.exp(scores - row_top)
    attn_prob = weight / lax.optimization_barrier(jnp.sum(weight, axis=-1, keepdims=True))
    rounded = lax.optimization_barrier(attn_prob.astype(jnp.bfloat16))
    mixture = jnp.einsum('...hpr,...rhd->...phd', rounded.astype(jnp.float32), values.astype(jnp.float32)).astype(jnp.bfloat16)
    return (mixture.reshape(leading + (WT, features)), (queries, key_heads, values, attn_prob, rounded))

def attend_back(windows, qkv_weight, stored, delta_mixture):
    queries, key_heads, values, attn_prob, rounded = stored
    leading = windows.shape[:-2]
    features = windows.shape[-1]
    head_size = features // HEADS
    factor = head_size ** (-0.5)
    delta_heads = delta_mixture.reshape(leading + (WT, HEADS, head_size)).astype(jnp.float32)
    delta_probs = jnp.einsum('...phd,...rhd->...hpr', delta_heads, values.astype(jnp.float32))
    delta_values = jnp.einsum('...hpr,...phd->...rhd', rounded.astype(jnp.float32), delta_heads)
    delta_scores = attn_prob * (delta_probs - lax.optimization_barrier(jnp.sum(delta_probs * attn_prob, axis=-1, keepdims=True)))
    delta_low = lax.optimization_barrier(delta_scores.astype(jnp.bfloat16)).astype(jnp.float32)
    delta_query = jnp.einsum('...hpr,...rhd->...phd', delta_low, key_heads.astype(jnp.float32)) * factor
    delta_keys = jnp.einsum('...hpr,...phd->...rhd', delta_low, queries.astype(jnp.float32)) * factor
    delta_packed = jnp.stack((delta_query, delta_keys, delta_values), axis=-3).astype(jnp.bfloat16).reshape(-1, 3 * features)
    flattened = windows.reshape(-1, features)
    grad_qkv = jnp.dot(flattened.T, delta_packed, preferred_element_type=jnp.float32)
    delta_window = jnp.dot(delta_packed, qkv_weight.T, preferred_element_type=jnp.float32).astype(jnp.bfloat16)
    return (delta_window.reshape(leading + (WT, features)), grad_qkv, delta_scores)

def reference(tokens, gain_one, gain_two, qkv_weight, proj_weight, up_weight, down_weight, bias_table, pos_index, mask_ids, cotangent):
    levels, lat_rows, lon_cols, features = tokens.shape
    backward_shift = (-1, -(WLAT // 2), -(WLON // 2))
    forward_shift = (1, WLAT // 2, WLON // 2)
    normal_one, inverse_one = norm_stats(tokens)
    normed = (normal_one * gain_one).astype(jnp.bfloat16)
    windows = to_windows(jnp.roll(normed, backward_shift, (0, 1, 2)))
    mask_win = to_windows(mask_ids[..., None])[..., 0]
    bias_win = bias_pairs(bias_table, pos_index)

    def forward_row(member):
        mixture_row, stored = attend(member[0], member[1], member[2], qkv_weight)
        return mixture_row
    mixture = lax.map(forward_row, (windows, mask_win, bias_win))
    flat_mix = mixture.reshape(-1, features)
    attn_win = jnp.dot(flat_mix, proj_weight, preferred_element_type=jnp.float32).astype(jnp.bfloat16)
    attention = jnp.roll(from_windows(attn_win.reshape(mixture.shape), levels, lat_rows, lon_cols), forward_shift, (0, 1, 2))
    middle = (tokens.astype(jnp.float32) + attention.astype(jnp.float32)).astype(jnp.bfloat16)

    def mlp_level(member):
        return mlp_block(member[0].reshape(-1, features), gain_two, up_weight, down_weight, member[1].reshape(-1, features))
    output, delta_middle, gain_parts, up_parts, down_parts = lax.map(mlp_level, (middle, cotangent))
    output = output.reshape(tokens.shape)
    delta_middle = delta_middle.reshape(tokens.shape)
    grad_gain_two = lax.optimization_barrier(jnp.sum(gain_parts, axis=0))
    grad_up = lax.optimization_barrier(jnp.sum(up_parts, axis=0))
    grad_down = lax.optimization_barrier(jnp.sum(down_parts, axis=0))
    delta_attn = to_windows(jnp.roll(delta_middle, backward_shift, (0, 1, 2)))
    flat_delta = delta_attn.reshape(-1, features)
    grad_proj = jnp.dot(flat_mix.T, flat_delta, preferred_element_type=jnp.float32)
    delta_mixture = jnp.dot(flat_delta, proj_weight.T, preferred_element_type=jnp.float32).astype(jnp.bfloat16).reshape(mixture.shape)

    def backward_row(member):
        mixture_row, stored = attend(member[0], member[1], member[2], qkv_weight)
        delta_window, grad_part, delta_scores = attend_back(member[0], qkv_weight, stored, member[3])
        return (delta_window, grad_part, lax.optimization_barrier(jnp.sum(delta_scores, axis=1)))
    delta_window, qkv_parts, delta_type = lax.map(backward_row, (windows, mask_win, bias_win, delta_mixture))
    grad_qkv = lax.optimization_barrier(jnp.sum(qkv_parts, axis=0))
    grad_bias = table_grad(delta_type, pos_index)
    delta_normed = jnp.roll(from_windows(delta_window, levels, lat_rows, lon_cols), forward_shift, (0, 1, 2))
    delta_input, grad_gain_one = norm_back(delta_normed.astype(jnp.float32), normal_one, inverse_one, gain_one)
    delta_tokens = (delta_middle.astype(jnp.float32) + delta_input).astype(jnp.bfloat16)
    factor = TOKENS ** (-0.5)
    return (output, delta_tokens, grad_gain_one * factor, grad_gain_two * factor, grad_qkv * factor, grad_proj * factor, grad_up * factor, grad_down * factor, grad_bias)
```

```python
import jax
import jax.numpy as jnp
from jax import lax
from jax.experimental import pallas as pl
from jax.experimental.pallas import tpu as pltpu
from jax.sharding import PartitionSpec as P

HEADS = 6
WT = 144
NPOS = 3312
C = 192
HID = 768
HEAD = C // HEADS
SLOTS = 26
LANES = 128
TOKENS = 73728
TAIL = WT - LANES
ROWS = WT + 2 * TAIL
GROWS = 3584
BROWS = 160
EPS = 1e-05
F32 = jnp.float32
BF16 = jnp.bfloat16


def dot(a, b):
    return lax.dot_general(a, b, (((1,), (0,)), ((), ())), preferred_element_type=F32)


def dot_nt(a, b):
    return lax.dot_general(a, b, (((1,), (1,)), ((), ())), preferred_element_type=F32)


def dot_tn(a, b):
    return lax.dot_general(a, b, (((0,), (0,)), ((), ())), preferred_element_type=F32)


def norm_stats(widened):
    center = widened - jnp.mean(widened, axis=-1, keepdims=True)
    spread = jnp.mean(center * center, axis=-1, keepdims=True)
    inverse = lax.rsqrt(spread + EPS)
    return center * inverse, inverse


def norm_back(delta_hidden, normal, inverse, gain):
    grad_gain = jnp.sum(delta_hidden * normal, axis=0, keepdims=True)
    delta_normal = delta_hidden * gain
    delta_input = inverse * (
        delta_normal
        - jnp.mean(delta_normal, axis=-1, keepdims=True)
        - normal * jnp.mean(delta_normal * normal, axis=-1, keepdims=True)
    )
    return delta_input, grad_gain


def gather_kernel(table_ref, pos_ref, bias_ref, flat_ref):
    def rows(i, carry):
        at = pl.ds(pl.multiple_of(i * 8, 8), 8)
        pos = pos_ref[at, :]
        lane = jnp.bitwise_and(pos, LANES - 1)
        slot = jnp.right_shift(pos, 7)
        held = [jnp.zeros((8, LANES), F32)] * HEADS
        for g in range(SLOTS):
            here = slot == g
            for h in range(HEADS):
                row = jnp.broadcast_to(table_ref[h, g : g + 1, :], (8, LANES))
                got = jnp.take_along_axis(row, lane, axis=1)
                held[h] = jnp.where(here, got, held[h])
        for h in range(HEADS):
            flat_ref[h, at, :] = held[h]
        return carry

    lax.fori_loop(0, ROWS // 8, rows, 0)
    for h in range(HEADS):
        at = h * WT
        bias_ref[at : at + WT, :LANES] = flat_ref[h, :WT, :]
        bias_ref[at : at + LANES, LANES:] = flat_ref[h, WT : WT + TAIL, :].T
        bias_ref[at + LANES : at + WT, LANES:] = flat_ref[h, WT + TAIL :, :].T[:TAIL]


def bias_pairs(table, pos_flat):
    return pl.pallas_call(
        gather_kernel,
        out_shape=jax.ShapeDtypeStruct((HEADS * WT, WT), F32),
        scratch_shapes=[pltpu.VMEM((HEADS, ROWS, LANES), F32)],
        name="bias_pairs",
        compiler_params=pltpu.CompilerParams(vmem_limit_bytes=16 * 1024 * 1024),
        cost_estimate=pl.CostEstimate(flops=10_000_000, bytes_accessed=1_200_000, transcendentals=0),
    )(table, pos_flat)


def flat_pairs(pos_index):
    turned = pos_index[:, LANES:].T
    rest = jnp.pad(turned[:, LANES:], ((0, 0), (0, LANES - TAIL)))
    return jnp.concatenate((pos_index[:, :LANES], turned[:, :LANES], rest), axis=0)


def block_kernel(
    x_ref,
    cot_ref,
    gain_one_ref,
    gain_two_ref,
    qkv_ref,
    proj_ref,
    up_ref,
    down_ref,
    bias_ref,
    mask_row_ref,
    mask_col_ref,
    pos_ref,
    out_ref,
    delta_ref,
    grads_ref,
    grad_bias_ref,
    scores_ref,
    prob_ref,
    low_ref,
    pairs_ref,
    sums_ref,
):
    factor = HEAD ** (-0.5)
    x = x_ref[...].astype(F32)
    gain_one = gain_one_ref[...]
    gain_two = gain_two_ref[...]
    normal_one, inverse_one = norm_stats(x)
    normed = (normal_one * gain_one).astype(BF16)
    queries = dot(normed, qkv_ref[0]).astype(BF16)
    keys = dot(normed, qkv_ref[1]).astype(BF16)
    values = dot(normed, qkv_ref[2]).astype(BF16)
    head_of = lax.broadcasted_iota(jnp.int32, (WT, C), 1) // HEAD
    allowed = mask_col_ref[...] == mask_row_ref[...]

    def by_head(a):
        return jnp.concatenate([jnp.where(head_of == h, a, jnp.zeros_like(a)) for h in range(HEADS)], axis=0)

    def joined(a):
        out = a[:WT]
        for h in range(1, HEADS):
            out = jnp.where(head_of == h, a[h * WT : (h + 1) * WT], out)
        return out

    queries_by = by_head(queries)
    scores_ref[...] = dot_nt(queries_by, keys)
    for h in range(HEADS):
        at = pl.ds(h * WT, WT)
        scores = scores_ref[at, :] * factor + bias_ref[at, :]
        scores = jnp.where(allowed, scores, -1e30)
        weight = jnp.exp(scores - jnp.max(scores, axis=-1, keepdims=True))
        prob = weight * (1.0 / jnp.sum(weight, axis=-1, keepdims=True))
        prob_ref[at, :] = prob
        low_ref[at, :] = prob.astype(BF16)
    mixture = joined(dot(low_ref[...], values)).astype(BF16)
    attention = dot(mixture, proj_ref[...]).astype(BF16)

    middle = (x + attention.astype(F32)).astype(BF16)
    widened = middle.astype(F32)
    normal_two, inverse_two = norm_stats(widened)
    normed_two = (normal_two * gain_two).astype(BF16)
    cot = cot_ref[...]
    up_proj = dot(normed_two, up_ref[...])
    cumulative = 0.5 * (1.0 + lax.erf(up_proj * 0.7071067811865476))
    density = jnp.exp(-0.5 * up_proj * up_proj) * 0.3989422804014327
    active = (up_proj * cumulative).astype(BF16)
    out_ref[...] = (widened + dot(active, down_ref[...])).astype(BF16)
    grad_down = dot_tn(active, cot)
    grads_ref[1152:1920] = grad_down[:, :LANES].astype(BF16)
    grads_ref[1920:2304] = jnp.concatenate(
        (grad_down[:384, LANES:], grad_down[384:, LANES:]), axis=1
    ).astype(BF16)
    delta_act = dot_nt(cot, down_ref[...])
    delta_up = (delta_act * (cumulative + up_proj * density)).astype(BF16)
    grad_up = dot_tn(normed_two, delta_up).astype(BF16)
    for t in range(6):
        grads_ref[C * t : C * (t + 1)] = grad_up[:, LANES * t : LANES * (t + 1)]
    delta_hidden = dot_nt(delta_up, up_ref[...])
    delta_input, grad_gain_two = norm_back(delta_hidden, normal_two, inverse_two, gain_two)
    delta_middle = (cot.astype(F32) + delta_input).astype(BF16)

    grad_proj = dot_tn(mixture, delta_middle)
    mixture_by = by_head(dot_nt(delta_middle, proj_ref[...]).astype(BF16))
    delta_value = dot_tn(low_ref[...], mixture_by)
    scores_ref[...] = dot_nt(mixture_by, values)
    for h in range(HEADS):
        at = pl.ds(h * WT, WT)
        prob = prob_ref[at, :]
        delta_prob = scores_ref[at, :]
        scores = prob * (delta_prob - jnp.sum(delta_prob * prob, axis=-1, keepdims=True))
        low_ref[at, :] = scores.astype(BF16)
        turned = scores[:, LANES:].T
        pairs_ref[h, :WT, :] = scores[:, :LANES]
        pairs_ref[h, WT : WT + TAIL, :] = turned[:, :LANES]
        pairs_ref[h, WT + TAIL :, :] = jnp.zeros((TAIL, LANES), F32)
        pairs_ref[h, WT + TAIL :, :TAIL] = turned[:, LANES:]
    delta_query = joined(dot(low_ref[...], keys)) * factor
    delta_key = dot_tn(low_ref[...], queries_by) * factor
    delta_normed = jnp.zeros((WT, C), F32)
    parts = []
    for k, part in enumerate((delta_query, delta_key, delta_value)):
        part = part.astype(BF16)
        parts.append(dot_tn(normed, part))
        delta_normed = delta_normed + dot_nt(part, qkv_ref[k])
    parts.append(grad_proj)
    for k in range(4):
        grads_ref[2304 + C * k : 2304 + C * (k + 1)] = parts[k][:, :LANES].astype(BF16)
    for k in range(2):
        grads_ref[3072 + C * k : 3072 + C * (k + 1)] = jnp.concatenate(
            (parts[2 * k][:, LANES:], parts[2 * k + 1][:, LANES:]), axis=1
        ).astype(BF16)
    delta_normed = delta_normed.astype(BF16).astype(F32)
    delta_input, grad_gain_one = norm_back(delta_normed, normal_one, inverse_one, gain_one)
    delta_ref[...] = (delta_middle.astype(F32) + delta_input).astype(BF16)
    gains = jnp.concatenate((grad_gain_one, grad_gain_two), axis=0)
    wide = jnp.concatenate((gains, jnp.zeros((2, 2 * LANES - C), F32)), axis=1)
    grads_ref[3456:3584] = jnp.concatenate(
        (wide[:, :LANES], wide[:, LANES:], jnp.zeros((124, LANES), F32)), axis=0
    ).astype(BF16)

    sums_ref[...] = jnp.zeros_like(sums_ref)
    slot_ids = lax.broadcasted_iota(jnp.int32, (32, LANES), 0)
    lane_ids = lax.broadcasted_iota(jnp.int32, (LANES, LANES), 0)

    def rows(i, carry):
        spread, onehot = [], []
        for j in range(8):
            at = pl.ds(i * 8 + j, 1)
            pos = pos_ref[at, :]
            here = slot_ids == jnp.right_shift(pos, 7)
            lane = jnp.bitwise_and(pos, LANES - 1)
            onehot.append(jnp.where(lane_ids == lane, 1.0, 0.0).astype(BF16))
            spread.append(
                jnp.concatenate(
                    [jnp.where(here, pairs_ref[h, at, :], 0.0).astype(BF16) for h in range(HEADS)], axis=0
                )
            )
        sums_ref[...] += dot_nt(jnp.concatenate(spread, axis=1), jnp.concatenate(onehot, axis=1))
        return carry

    lax.fori_loop(0, ROWS // 8, rows, 0)
    grad_bias_ref[...] = sums_ref[...].astype(BF16)


def block(*args):
    shapes = [
        ((WT, C), BF16),
        ((WT, C), BF16),
        ((GROWS, LANES), BF16),
        ((HEADS * 32, LANES), BF16),
    ]
    return pl.pallas_call(
        block_kernel,
        out_shape=[jax.ShapeDtypeStruct(s, d) for s, d in shapes],
        scratch_shapes=[
            pltpu.VMEM((HEADS * WT, WT), F32),
            pltpu.VMEM((HEADS * WT, WT), F32),
            pltpu.VMEM((HEADS * WT, WT), BF16),
            pltpu.VMEM((HEADS, ROWS, LANES), F32),
            pltpu.VMEM((HEADS * 32, LANES), F32),
        ],
        name="block",
        compiler_params=pltpu.CompilerParams(vmem_limit_bytes=24 * 1024 * 1024),
        cost_estimate=pl.CostEstimate(flops=2_000_000_000, bytes_accessed=5_000_000, transcendentals=300_000),
    )(*args)


def unpack_kernel(grads_ref, gain_one_ref, gain_two_ref, qkv_ref, proj_ref, up_ref, down_ref):
    factor = TOKENS ** (-0.5)

    def rows(start, count):
        return grads_ref[start : start + count].astype(F32) * factor

    for t in range(6):
        up_ref[:, LANES * t : LANES * (t + 1)] = rows(C * t, C)
    half = rows(1920, 384)
    down_ref[:, :LANES] = rows(1152, 768)
    down_ref[:384, LANES:] = half[:, :64]
    down_ref[384:, LANES:] = half[:, 64:]
    full = [rows(2304 + C * k, C) for k in range(4)]
    halves = [rows(3072 + C * k, C) for k in range(2)]
    query, key, value, proj = [
        jnp.concatenate((full[k], halves[k // 2][:, 64 * (k % 2) : 64 * (k % 2 + 1)]), axis=1) for k in range(4)
    ]
    qkv_ref[...] = jnp.concatenate((query, key, value), axis=1)
    proj_ref[...] = proj
    gains = rows(3456, 16)
    for k, ref in enumerate((gain_one_ref, gain_two_ref)):
        ref[...] = jnp.concatenate((gains[k : k + 1], gains[k + 2 : k + 3, : C - LANES]), axis=1)


def unpack(grads):
    shapes = [(1, C), (1, C), (C, 3 * C), (C, C), (C, HID), (HID, C)]
    return pl.pallas_call(
        unpack_kernel,
        out_shape=[jax.ShapeDtypeStruct(s, F32) for s in shapes],
        name="unpack",
        compiler_params=pltpu.CompilerParams(vmem_limit_bytes=16 * 1024 * 1024),
        cost_estimate=pl.CostEstimate(flops=500_000, bytes_accessed=2_700_000, transcendentals=0),
    )(grads)


def neighbours(by):
    lat, lon = lax.axis_size("lat"), lax.axis_size("lon")
    return [
        (i * lon + j, (i + by) % lat * lon + (j + by) % lon) for i in range(lat) for j in range(lon)
    ]


def ring(axis, by):
    peers = lax.axis_size(axis)
    return [(i, (i + by) % peers) for i in range(peers)]


def shift_in(grid):
    from_lat = lax.ppermute(grid[:, :, :3, 6:], "lat", ring("lat", -1))
    from_lon = lax.ppermute(grid[:, :, 3:, :6], "lon", ring("lon", -1))
    from_both = lax.ppermute(grid[:, :, :3, :6], ("lat", "lon"), neighbours(-1))
    top = jnp.concatenate((grid[:, :, 3:, 6:], from_lon), axis=3)
    low = jnp.concatenate((from_lat, from_both), axis=3)
    return jnp.concatenate((top, low), axis=2)[:, ::-1]


def shift_out(grid, between):
    rows_got = lax.ppermute(grid[:, :, 3:], "lat", ring("lat", 1))
    between(0)
    grid = jnp.concatenate((rows_got, grid[:, :, :3]), axis=2)
    cols_got = lax.ppermute(grid[:, :, :, 6:], "lon", ring("lon", 1))
    between(1)
    return jnp.concatenate((cols_got, grid[:, :, :, :6]), axis=3)


def spread_over(axis, groups=None):
    return lambda parts: lax.all_to_all(parts, axis, 0, 0, axis_index_groups=groups)


def total(parts):
    return jnp.sum(parts.astype(F32), axis=0).astype(BF16)


def reduce_grads(grads, local_bias):
    lat, lon = lax.axis_size("lat"), lax.axis_size("lon")
    far = 4
    near = lon // far
    over_near = spread_over("lon", [[n * far + f for n in range(near)] for f in range(far)])
    over_far = spread_over("lon", [[n * far + f for f in range(far)] for n in range(near)])
    over_lat = spread_over("lat")

    def same(part, count):
        return jnp.broadcast_to(part[None], (count,) + part.shape)

    share = GROWS // lat
    mine = total(over_lat(grads.reshape(lat, share, LANES)))
    both = jnp.concatenate((mine, local_bias), axis=0)
    part = total(over_near(both.reshape(near, -1, LANES)))
    part = total(over_far(same(part, far)))
    both = over_near(same(part, near)).reshape(both.shape)
    grads = over_lat(same(both[:share], lat)).reshape(GROWS, LANES)
    return grads, both[share:]


def local(
    tokens,
    gain_one,
    gain_two,
    qkv_weight,
    proj_weight,
    up_weight,
    down_weight,
    bias_table,
    pos_index,
    mask_ids,
    cotangent,
):
    grid = tokens.shape
    moved = shift_in(jnp.stack((tokens, cotangent)))
    pos_flat = flat_pairs(pos_index)
    table = jnp.pad(bias_table.reshape(HEADS, NPOS), ((0, 0), (0, SLOTS * LANES - NPOS)))
    bias = bias_pairs(table.reshape(HEADS, SLOTS, LANES), pos_flat)
    weights = qkv_weight.reshape(C, 3, C).transpose(1, 0, 2)
    out, delta, grads, local_bias = block(
        moved[0].reshape(WT, C),
        moved[1].reshape(WT, C),
        gain_one.reshape(1, C),
        gain_two.reshape(1, C),
        weights,
        proj_weight,
        up_weight,
        down_weight,
        bias,
        mask_ids.reshape(1, WT),
        mask_ids.reshape(WT, 1),
        pos_flat,
    )
    back = shift_out(jnp.stack((out, delta)).reshape((2,) + grid)[:, ::-1], lambda stage: None)
    local_bias = local_bias.reshape(HEADS, 32, LANES)[:, :SLOTS].reshape(HEADS * SLOTS, LANES)
    grads, grad_bias = reduce_grads(grads, jnp.pad(local_bias, ((0, BROWS - HEADS * SLOTS), (0, 0))))
    totals = unpack(grads)
    grad_bias = grad_bias[: HEADS * SLOTS].reshape(HEADS, SLOTS * LANES)[:, :NPOS].astype(F32)
    return (
        back[0],
        back[1],
        totals[0].reshape(C),
        totals[1].reshape(C),
        *totals[2:],
        grad_bias.reshape(HEADS, 1, 1, NPOS),
    )


def solution(mesh):
    in_specs = (
        P(None, "lat", "lon", None),
        P(),
        P(),
        P(),
        P(),
        P(),
        P(),
        P(None, None, "lat", None),
        P(),
        P(None, "lat", "lon"),
        P(None, "lat", "lon", None),
    )
    out_specs = (
        P(None, "lat", "lon", None),
        P(None, "lat", "lon", None),
        P(),
        P(),
        P(),
        P(),
        P(),
        P(),
        P(None, None, "lat", None),
    )
    return jax.shard_map(local, mesh=mesh, in_specs=in_specs, out_specs=out_specs, check_vma=False)
```

```python
import jax
import jax.numpy as jnp
from jax import lax
from jax.experimental import pallas as pl
from jax.experimental.pallas import tpu as pltpu
from jax.sharding import PartitionSpec as P

HEADS = 6
WT = 144
NPOS = 3312
C = 192
HID = 768
HEAD = C // HEADS
SLOTS = 26
LANES = 128
TOKENS = 73728
TAIL = WT - LANES
ROWS = WT + 2 * TAIL
GROWS = 3584
BROWS = 160
EPS = 1e-05
F32 = jnp.float32
BF16 = jnp.bfloat16


def dot(a, b):
    return lax.dot_general(a, b, (((1,), (0,)), ((), ())), preferred_element_type=F32)


def dot_nt(a, b):
    return lax.dot_general(a, b, (((1,), (1,)), ((), ())), preferred_element_type=F32)


def dot_tn(a, b):
    return lax.dot_general(a, b, (((0,), (0,)), ((), ())), preferred_element_type=F32)


def norm_stats(widened):
    center = widened - jnp.mean(widened, axis=-1, keepdims=True)
    spread = jnp.mean(center * center, axis=-1, keepdims=True)
    inverse = lax.rsqrt(spread + EPS)
    return center * inverse, inverse


def norm_back(delta_hidden, normal, inverse, gain):
    grad_gain = jnp.sum(delta_hidden * normal, axis=0, keepdims=True)
    delta_normal = delta_hidden * gain
    delta_input = inverse * (
        delta_normal
        - jnp.mean(delta_normal, axis=-1, keepdims=True)
        - normal * jnp.mean(delta_normal * normal, axis=-1, keepdims=True)
    )
    return delta_input, grad_gain


def gather_kernel(table_ref, pos_ref, mask_ref, bias_ref, flat_pos_ref, slots_ref, flat_ref):
    half = WT // 2
    pos = pos_ref[...]
    pos = jnp.concatenate((pos[half:], pos[:half]), axis=0)
    pos = jnp.concatenate((pos[:, half:], pos[:, :half]), axis=1)
    turned = pos[:, LANES:].T
    flat_pos_ref[:WT] = pos[:, :LANES]
    flat_pos_ref[WT : WT + TAIL] = turned[:, :LANES]
    flat_pos_ref[WT + TAIL :] = jnp.zeros((TAIL, LANES), jnp.int32)
    flat_pos_ref[WT + TAIL :, :TAIL] = turned[:, LANES:]
    for h in range(HEADS):
        for g in range(SLOTS):
            count = min(LANES, NPOS - g * LANES)
            slots_ref[h, g : g + 1, :count] = table_ref[h, :, g * LANES : g * LANES + count]

    def rows(i, carry):
        at = pl.ds(pl.multiple_of(i * 8, 8), 8)
        pos = flat_pos_ref[at, :]
        lane = jnp.bitwise_and(pos, LANES - 1)
        slot = jnp.right_shift(pos, 7)
        held = [jnp.zeros((8, LANES), F32)] * HEADS
        for g in range(SLOTS):
            here = slot == g
            for h in range(HEADS):
                row = jnp.broadcast_to(slots_ref[h, g : g + 1, :], (8, LANES))
                got = jnp.take_along_axis(row, lane, axis=1)
                held[h] = jnp.where(here, got, held[h])
        for h in range(HEADS):
            flat_ref[h, at, :] = held[h]
        return carry

    lax.fori_loop(0, ROWS // 8, rows, 0)
    mask = jnp.broadcast_to(mask_ref[...], (WT, WT))
    allowed = mask == mask.T
    for h in range(HEADS):
        tail = jnp.concatenate((flat_ref[h, WT : WT + TAIL, :].T, flat_ref[h, WT + TAIL :, :].T[:TAIL]), axis=0)
        at = pl.ds(h * WT, WT)
        bias_ref[at, :LANES] = jnp.where(allowed[:, :LANES], flat_ref[h, :WT, :], -1e30)
        bias_ref[at, LANES:] = jnp.where(allowed[:, LANES:], tail, -1e30)


def bias_pairs(table, pos_index, mask_row):
    return pl.pallas_call(
        gather_kernel,
        out_shape=[jax.ShapeDtypeStruct((HEADS * WT, WT), F32), jax.ShapeDtypeStruct((ROWS, LANES), jnp.int32)],
        scratch_shapes=[pltpu.VMEM((HEADS, SLOTS, LANES), F32), pltpu.VMEM((HEADS, ROWS, LANES), F32)],
        name="bias_pairs",
        compiler_params=pltpu.CompilerParams(vmem_limit_bytes=16 * 1024 * 1024),
        cost_estimate=pl.CostEstimate(flops=10_000_000, bytes_accessed=1_200_000, transcendentals=0),
    )(table, pos_index, mask_row)


def scatter_kernel(pairs_ref, pos_ref, out_ref, sums_ref, packed_ref):
    sums_ref[...] = jnp.zeros_like(sums_ref)
    slot_ids = lax.broadcasted_iota(jnp.int32, (32, LANES), 0)
    lane_ids = lax.broadcasted_iota(jnp.int32, (LANES, LANES), 0)

    def rows(i, carry):
        spread, onehot = [], []
        for j in range(8):
            at = pl.ds(i * 8 + j, 1)
            pos = pos_ref[at, :]
            here = slot_ids == jnp.right_shift(pos, 7)
            lane = jnp.bitwise_and(pos, LANES - 1)
            onehot.append(jnp.where(lane_ids == lane, 1.0, 0.0).astype(BF16))
            spread.append(
                jnp.concatenate(
                    [jnp.where(here, pairs_ref[h, at, :], 0.0).astype(BF16) for h in range(HEADS)], axis=0
                )
            )
        sums_ref[...] += dot_nt(jnp.concatenate(spread, axis=1), jnp.concatenate(onehot, axis=1))
        return carry

    lax.fori_loop(0, ROWS // 8, rows, 0)
    packed_ref[...] = jnp.zeros_like(packed_ref)
    for h in range(HEADS):
        packed_ref[h * SLOTS : (h + 1) * SLOTS] = sums_ref[h * 32 : h * 32 + SLOTS]
    out_ref[...] = packed_ref[...].astype(BF16)


def bias_grad(pairs, pos_flat):
    return pl.pallas_call(
        scatter_kernel,
        out_shape=jax.ShapeDtypeStruct((BROWS, LANES), BF16),
        scratch_shapes=[pltpu.VMEM((HEADS * 32, LANES), F32), pltpu.VMEM((BROWS, LANES), F32)],
        name="bias_grad",
        compiler_params=pltpu.CompilerParams(vmem_limit_bytes=16 * 1024 * 1024),
        cost_estimate=pl.CostEstimate(flops=1_100_000_000, bytes_accessed=700_000, transcendentals=0),
    )(pairs, pos_flat)


def block_kernel(
    x_ref,
    cot_ref,
    gain_one_ref,
    gain_two_ref,
    qkv_ref,
    proj_ref,
    up_ref,
    down_ref,
    bias_ref,
    out_ref,
    delta_ref,
    grads_ref,
    pairs_ref,
    scores_ref,
    prob_ref,
    low_ref,
):
    factor = HEAD ** (-0.5)
    x = x_ref[...].astype(F32)
    gain_one = gain_one_ref[...]
    gain_two = gain_two_ref[...]
    normal_one, inverse_one = norm_stats(x)
    normed = (normal_one * gain_one).astype(BF16)
    packed = dot(normed, qkv_ref[...]).astype(BF16)
    queries, keys, values = packed[:, :C], packed[:, C : 2 * C], packed[:, 2 * C :]
    head_of = lax.broadcasted_iota(jnp.int32, (WT, C), 1) // HEAD

    def by_head(a):
        return jnp.concatenate([jnp.where(head_of == h, a, jnp.zeros_like(a)) for h in range(HEADS)], axis=0)

    def joined(a):
        out = a[:WT]
        for h in range(1, HEADS):
            out = jnp.where(head_of == h, a[h * WT : (h + 1) * WT], out)
        return out

    queries_by = by_head(queries)
    scores_ref[...] = dot_nt(queries_by, keys)
    for h in range(HEADS):
        at = pl.ds(h * WT, WT)
        scores = scores_ref[at, :] * factor + bias_ref[at, :]
        weight = jnp.exp(scores - jnp.max(scores, axis=-1, keepdims=True))
        prob = weight * (1.0 / jnp.sum(weight, axis=-1, keepdims=True))
        prob_ref[at, :] = prob
        low_ref[at, :] = prob.astype(BF16)
    mixture = joined(dot(low_ref[...], values)).astype(BF16)
    attention = dot(mixture, proj_ref[...]).astype(BF16)

    middle = (x + attention.astype(F32)).astype(BF16)
    widened = middle.astype(F32)
    normal_two, inverse_two = norm_stats(widened)
    normed_two = (normal_two * gain_two).astype(BF16)
    cot = cot_ref[...]
    up_proj = dot(normed_two, up_ref[...])
    cumulative = 0.5 * (1.0 + lax.erf(up_proj * 0.7071067811865476))
    density = jnp.exp(-0.5 * up_proj * up_proj) * 0.3989422804014327
    active = (up_proj * cumulative).astype(BF16)
    out_ref[...] = (widened + dot_nt(active, down_ref[...])).astype(BF16)
    grad_down = dot_tn(cot, active).astype(BF16)
    delta_act = dot(cot, down_ref[...])
    delta_up = (delta_act * (cumulative + up_proj * density)).astype(BF16)
    grad_up = dot_tn(normed_two, delta_up).astype(BF16)
    for t in range(6):
        grads_ref[C * t : C * (t + 1)] = grad_up[:, LANES * t : LANES * (t + 1)]
        grads_ref[C * (t + 6) : C * (t + 7)] = grad_down[:, LANES * t : LANES * (t + 1)]
    delta_hidden = dot_nt(delta_up, up_ref[...])
    delta_input, grad_gain_two = norm_back(delta_hidden, normal_two, inverse_two, gain_two)
    delta_middle = (cot.astype(F32) + delta_input).astype(BF16)

    grad_proj = dot_tn(mixture, delta_middle)
    mixture_by = by_head(dot_nt(delta_middle, proj_ref[...]).astype(BF16))
    delta_value = dot_tn(low_ref[...], mixture_by)
    scores_ref[...] = dot_nt(mixture_by, values)
    for h in range(HEADS):
        at = pl.ds(h * WT, WT)
        prob = prob_ref[at, :]
        delta_prob = scores_ref[at, :]
        scores = prob * (delta_prob - jnp.sum(delta_prob * prob, axis=-1, keepdims=True))
        low_ref[at, :] = scores.astype(BF16)
        turned = scores[:, LANES:].T
        pairs_ref[h, :WT, :] = scores[:, :LANES]
        pairs_ref[h, WT : WT + TAIL, :] = turned[:, :LANES]
        pairs_ref[h, WT + TAIL :, :] = jnp.zeros((TAIL, LANES), F32)
        pairs_ref[h, WT + TAIL :, :TAIL] = turned[:, LANES:]
    delta_query = joined(dot(low_ref[...], keys)) * factor
    delta_key = dot_tn(low_ref[...], queries_by) * factor
    delta_packed = jnp.concatenate((delta_query, delta_key, delta_value), axis=1).astype(BF16)
    delta_normed = dot_nt(delta_packed, qkv_ref[...])
    grad_qkv = dot_tn(normed, delta_packed)
    for t in range(4):
        grads_ref[C * (t + 12) : C * (t + 13)] = grad_qkv[:, LANES * t : LANES * (t + 1)].astype(BF16)
    grads_ref[C * 16 : C * 17] = grad_proj[:, :LANES].astype(BF16)
    grads_ref[C * 17 : C * 18] = jnp.concatenate((grad_qkv[:, 4 * LANES :], grad_proj[:, LANES:]), axis=1).astype(BF16)
    delta_normed = delta_normed.astype(BF16).astype(F32)
    delta_input, grad_gain_one = norm_back(delta_normed, normal_one, inverse_one, gain_one)
    delta_ref[...] = (delta_middle.astype(F32) + delta_input).astype(BF16)
    gains = jnp.concatenate((grad_gain_one, grad_gain_two), axis=0)
    wide = jnp.concatenate((gains, jnp.zeros((2, 2 * LANES - C), F32)), axis=1)
    grads_ref[C * 18 :] = jnp.concatenate(
        (wide[:, :LANES], wide[:, LANES:], jnp.zeros((124, LANES), F32)), axis=0
    ).astype(BF16)


def block(*args):
    shapes = [
        ((WT, C), BF16),
        ((WT, C), BF16),
        ((GROWS, LANES), BF16),
        ((HEADS, ROWS, LANES), F32),
    ]
    return pl.pallas_call(
        block_kernel,
        out_shape=[jax.ShapeDtypeStruct(s, d) for s, d in shapes],
        scratch_shapes=[
            pltpu.VMEM((HEADS * WT, WT), F32),
            pltpu.VMEM((HEADS * WT, WT), F32),
            pltpu.VMEM((HEADS * WT, WT), BF16),
        ],
        name="block",
        compiler_params=pltpu.CompilerParams(vmem_limit_bytes=24 * 1024 * 1024),
        cost_estimate=pl.CostEstimate(flops=900_000_000, bytes_accessed=4_000_000, transcendentals=300_000),
    )(*args)


def unpack_kernel(grads_ref, gain_one_ref, gain_two_ref, qkv_ref, proj_ref, up_ref, down_ref):
    factor = TOKENS ** (-0.5)

    def rows(start, count):
        return grads_ref[start : start + count].astype(F32) * factor

    for t in range(6):
        at = slice(LANES * t, LANES * (t + 1))
        up_ref[:, at] = rows(C * t, C)
        down_ref[:, at] = rows(C * (t + 6), C)
        if t < 4:
            qkv_ref[:, at] = rows(C * (t + 12), C)
    halves = rows(C * 17, C)
    qkv_ref[:, 4 * LANES :] = halves[:, :64]
    proj_ref[:, :LANES] = rows(C * 16, C)
    proj_ref[:, LANES:] = halves[:, 64:]
    gains = rows(C * 18, 16)
    for k, ref in enumerate((gain_one_ref, gain_two_ref)):
        ref[...] = jnp.concatenate((gains[k : k + 1], gains[k + 2 : k + 3, : C - LANES]), axis=1)


def unpack(grads):
    shapes = [(1, C), (1, C), (C, 3 * C), (C, C), (C, HID), (C, HID)]
    return pl.pallas_call(
        unpack_kernel,
        out_shape=[jax.ShapeDtypeStruct(s, F32) for s in shapes],
        name="unpack",
        compiler_params=pltpu.CompilerParams(vmem_limit_bytes=16 * 1024 * 1024),
        cost_estimate=pl.CostEstimate(flops=500_000, bytes_accessed=2_700_000, transcendentals=0),
    )(grads)


def neighbours(by):
    lat, lon = lax.axis_size("lat"), lax.axis_size("lon")
    return [
        (i * lon + j, (i + by) % lat * lon + (j + by) % lon) for i in range(lat) for j in range(lon)
    ]


def ring(axis, by):
    peers = lax.axis_size(axis)
    return [(i, (i + by) % peers) for i in range(peers)]


def shift_in(grid):
    from_lat = lax.ppermute(grid[:, :, :3, 6:], "lat", ring("lat", -1))
    from_lon = lax.ppermute(grid[:, :, 3:, :6], "lon", ring("lon", -1))
    from_both = lax.ppermute(grid[:, :, :3, :6], ("lat", "lon"), neighbours(-1))
    top = jnp.concatenate((grid[:, :, 3:, 6:], from_lon), axis=3)
    low = jnp.concatenate((from_lat, from_both), axis=3)
    return jnp.concatenate((top, low), axis=2)


def spread_over(axis, groups=None):
    return lambda parts: lax.all_to_all(parts, axis, 0, 0, axis_index_groups=groups)


def total(parts):
    return jnp.sum(parts.astype(F32), axis=0).astype(BF16)


def finish(grid, grads, pairs, pos_flat):
    lat, lon = lax.axis_size("lat"), lax.axis_size("lon")
    far = 4
    near = lon // far
    over_near = spread_over("lon", [[n * far + f for n in range(near)] for f in range(far)])
    over_far = spread_over("lon", [[n * far + f for f in range(far)] for n in range(near)])
    over_lat = spread_over("lat")

    def same(part, count):
        return jnp.broadcast_to(part[None], (count,) + part.shape)

    share = GROWS // lat
    mine = total(over_lat(grads.reshape(lat, share, LANES)))
    both = jnp.concatenate((mine, bias_grad(pairs, pos_flat)), axis=0)
    both, grid = lax.optimization_barrier((both, grid))
    rows_got = lax.ppermute(grid[:, :, 3:], "lat", ring("lat", 1))
    part = total(over_near(both.reshape(near, -1, LANES)))
    part = total(over_far(same(part, far)))
    part, rows_got = lax.optimization_barrier((part, rows_got))
    grid = jnp.concatenate((rows_got, grid[:, :, :3]), axis=2)
    cols_got = lax.ppermute(grid[:, :, :, 6:], "lon", ring("lon", 1))
    both = over_near(same(part, near)).reshape(both.shape)
    both, cols_got = lax.optimization_barrier((both, cols_got))
    grid = jnp.concatenate((cols_got, grid[:, :, :, :6]), axis=3)
    grads = over_lat(same(both[:share], lat)).reshape(GROWS, LANES)
    return grid, grads, both[share:]


def local(
    tokens,
    gain_one,
    gain_two,
    qkv_weight,
    proj_weight,
    up_weight,
    down_weight,
    bias_table,
    pos_index,
    mask_ids,
    cotangent,
):
    grid = tokens.shape
    moved = shift_in(jnp.stack((tokens, cotangent)))
    bias, pos_flat = bias_pairs(bias_table.reshape(HEADS, 1, NPOS), pos_index, mask_ids[::-1].reshape(1, WT))
    out, delta, grads, pairs = block(
        moved[0].reshape(WT, C),
        moved[1].reshape(WT, C),
        gain_one.reshape(1, C),
        gain_two.reshape(1, C),
        qkv_weight,
        proj_weight,
        up_weight,
        down_weight.T,
        bias,
    )
    back, grads, grad_bias = finish(jnp.stack((out, delta)).reshape((2,) + grid), grads, pairs, pos_flat)
    totals = unpack(grads)
    grad_bias = grad_bias[: HEADS * SLOTS].reshape(HEADS, SLOTS * LANES)[:, :NPOS].astype(F32)
    return (
        back[0],
        back[1],
        totals[0].reshape(C),
        totals[1].reshape(C),
        *totals[2:5],
        totals[5].T,
        grad_bias.reshape(HEADS, 1, 1, NPOS),
    )


def solution(mesh):
    in_specs = (
        P(None, "lat", "lon", None),
        P(),
        P(),
        P(),
        P(),
        P(),
        P(),
        P(None, None, "lat", None),
        P(),
        P(None, "lat", "lon"),
        P(None, "lat", "lon", None),
    )
    out_specs = (
        P(None, "lat", "lon", None),
        P(None, "lat", "lon", None),
        P(),
        P(),
        P(),
        P(),
        P(),
        P(),
        P(None, None, "lat", None),
    )
    return jax.shard_map(local, mesh=mesh, in_specs=in_specs, out_specs=out_specs, check_vma=False)
```

```python
import jax
import jax.numpy as jnp
from jax import lax
from jax.experimental import pallas as pl
from jax.experimental.pallas import tpu as pltpu
from jax.sharding import PartitionSpec as P

HEADS = 6
WT = 144
NPOS = 3312
C = 192
HID = 768
HEAD = C // HEADS
SLOTS = 26
LANES = 128
TOKENS = 73728
TAIL = WT - LANES
ROWS = WT + 2 * TAIL
GROWS = 3584
STEP = 44
BROWS = 160
EPS = 1e-05
F32 = jnp.float32
BF16 = jnp.bfloat16


def dot(a, b):
    return lax.dot_general(a, b, (((1,), (0,)), ((), ())), preferred_element_type=F32)


def dot_nt(a, b):
    return lax.dot_general(a, b, (((1,), (1,)), ((), ())), preferred_element_type=F32)


def dot_tn(a, b):
    return lax.dot_general(a, b, (((0,), (0,)), ((), ())), preferred_element_type=F32)


def norm_stats(widened):
    center = widened - jnp.mean(widened, axis=-1, keepdims=True)
    spread = jnp.mean(center * center, axis=-1, keepdims=True)
    inverse = lax.rsqrt(spread + EPS)
    return center * inverse, inverse


def norm_back(delta_hidden, normal, inverse, gain):
    grad_gain = jnp.sum(delta_hidden * normal, axis=0, keepdims=True)
    delta_normal = delta_hidden * gain
    delta_input = inverse * (
        delta_normal
        - jnp.mean(delta_normal, axis=-1, keepdims=True)
        - normal * jnp.mean(delta_normal * normal, axis=-1, keepdims=True)
    )
    return delta_input, grad_gain


def gather_kernel(table_ref, pos_ref, mask_ref, bias_ref, flat_pos_ref, slots_ref, flat_ref):
    half = WT // 2
    pos = pos_ref[...]
    pos = jnp.concatenate((pos[half:], pos[:half]), axis=0)
    pos = jnp.concatenate((pos[:, half:], pos[:, :half]), axis=1)
    turned = pos[:, LANES:].T
    flat_pos_ref[:WT] = pos[:, :LANES]
    flat_pos_ref[WT : WT + TAIL] = turned[:, :LANES]
    flat_pos_ref[WT + TAIL :] = jnp.zeros((TAIL, LANES), jnp.int32)
    flat_pos_ref[WT + TAIL :, :TAIL] = turned[:, LANES:]
    for h in range(HEADS):
        for g in range(SLOTS):
            count = min(LANES, NPOS - g * LANES)
            row = table_ref[h, :, g * LANES : g * LANES + count]
            slots_ref[h, g, :, :count] = jnp.broadcast_to(row, (8, count))

    def rows(i, carry):
        ats = [pl.ds(pl.multiple_of(i * 16 + 8 * k, 8), 8) for k in range(2)]
        pos = [flat_pos_ref[at, :] for at in ats]
        lane = [jnp.bitwise_and(p, LANES - 1) for p in pos]
        slot = [jnp.right_shift(p, 7) for p in pos]
        held = [[jnp.zeros((8, LANES), F32)] * HEADS for _ in ats]
        for g in range(SLOTS):
            here = [s == g for s in slot]
            for h in range(HEADS):
                row = slots_ref[h, g]
                for k in range(2):
                    got = jnp.take_along_axis(row, lane[k], axis=1)
                    held[k][h] = jnp.where(here[k], got, held[k][h])
        for k, at in enumerate(ats):
            for h in range(HEADS):
                flat_ref[h, at, :] = held[k][h]
        return carry

    lax.fori_loop(0, ROWS // 16, rows, 0)
    mask = jnp.broadcast_to(mask_ref[...], (WT, WT))
    allowed = mask == mask.T
    for h in range(HEADS):
        tail = jnp.concatenate((flat_ref[h, WT : WT + TAIL, :].T, flat_ref[h, WT + TAIL :, :].T[:TAIL]), axis=0)
        at = pl.ds(h * WT, WT)
        bias_ref[at, :LANES] = jnp.where(allowed[:, :LANES], flat_ref[h, :WT, :], -1e30)
        bias_ref[at, LANES:] = jnp.where(allowed[:, LANES:], tail, -1e30)


def bias_pairs(table, pos_index, mask_row):
    return pl.pallas_call(
        gather_kernel,
        out_shape=[jax.ShapeDtypeStruct((HEADS * WT, WT), F32), jax.ShapeDtypeStruct((ROWS, LANES), jnp.int32)],
        scratch_shapes=[pltpu.VMEM((HEADS, SLOTS, 8, LANES), F32), pltpu.VMEM((HEADS, ROWS, LANES), F32)],
        name="bias_pairs",
        compiler_params=pltpu.CompilerParams(vmem_limit_bytes=16 * 1024 * 1024),
        cost_estimate=pl.CostEstimate(flops=10_000_000, bytes_accessed=1_200_000, transcendentals=0),
    )(table, pos_index, mask_row)


def scatter_kernel(pairs_ref, pos_ref, out_ref, sums_ref, packed_ref):
    sums_ref[...] = jnp.zeros_like(sums_ref)
    slot_ids = lax.broadcasted_iota(jnp.int32, (32, LANES), 0)
    lane_ids = lax.broadcasted_iota(jnp.int32, (LANES, LANES), 0)

    def rows(i, carry):
        spread, onehot = [], []
        for j in range(STEP):
            at = pl.ds(i * STEP + j, 1)
            pos = pos_ref[at, :]
            slot = jnp.where(slot_ids == jnp.right_shift(pos, 7), 1.0, 0.0).astype(BF16)
            lane = jnp.bitwise_and(pos, LANES - 1)
            onehot.append(jnp.where(lane_ids == lane, 1.0, 0.0).astype(BF16))
            spread.append(
                jnp.concatenate(
                    [slot * jnp.broadcast_to(pairs_ref[h, at, :], (32, LANES)).astype(BF16) for h in range(HEADS)],
                    axis=0,
                )
            )
        sums_ref[...] += dot_nt(jnp.concatenate(spread, axis=1), jnp.concatenate(onehot, axis=1))
        return carry

    lax.fori_loop(0, ROWS // STEP, rows, 0)
    packed_ref[...] = jnp.zeros_like(packed_ref)
    for h in range(HEADS):
        packed_ref[h * SLOTS : (h + 1) * SLOTS] = sums_ref[h * 32 : h * 32 + SLOTS]
    out_ref[...] = packed_ref[...].astype(BF16)


def bias_grad(pairs, pos_flat):
    return pl.pallas_call(
        scatter_kernel,
        out_shape=jax.ShapeDtypeStruct((BROWS, LANES), BF16),
        scratch_shapes=[pltpu.VMEM((HEADS * 32, LANES), F32), pltpu.VMEM((BROWS, LANES), F32)],
        name="bias_grad",
        compiler_params=pltpu.CompilerParams(vmem_limit_bytes=16 * 1024 * 1024),
        cost_estimate=pl.CostEstimate(flops=1_100_000_000, bytes_accessed=700_000, transcendentals=0),
    )(pairs, pos_flat)


def block_kernel(
    x_ref,
    cot_ref,
    gains_ref,
    qkv_ref,
    proj_ref,
    up_ref,
    down_ref,
    bias_ref,
    out_ref,
    delta_ref,
    grads_ref,
    pairs_ref,
    scores_ref,
    prob_ref,
    low_ref,
):
    factor = HEAD ** (-0.5)
    x = x_ref[...].astype(F32)
    gain_one, gain_two = gains_ref[0:1], gains_ref[1:2]
    normal_one, inverse_one = norm_stats(x)
    normed = (normal_one * gain_one).astype(BF16)
    packed = dot(normed, qkv_ref[...]).astype(BF16)
    queries, keys, values = packed[:, :C], packed[:, C : 2 * C], packed[:, 2 * C :]
    head_of = lax.broadcasted_iota(jnp.int32, (WT, C), 1) // HEAD

    def by_head(a):
        return jnp.concatenate([jnp.where(head_of == h, a, jnp.zeros_like(a)) for h in range(HEADS)], axis=0)

    def joined(a):
        out = a[:WT]
        for h in range(1, HEADS):
            out = jnp.where(head_of == h, a[h * WT : (h + 1) * WT], out)
        return out

    queries_by = by_head(queries)
    scores_ref[...] = dot_nt(queries_by, keys)
    for h in range(HEADS):
        at = pl.ds(h * WT, WT)
        scores = scores_ref[at, :] * factor + bias_ref[at, :]
        weight = jnp.exp(scores - jnp.max(scores, axis=-1, keepdims=True))
        prob = weight * (1.0 / jnp.sum(weight, axis=-1, keepdims=True))
        prob_ref[at, :] = prob
        low_ref[at, :] = prob.astype(BF16)
    mixture = joined(dot(low_ref[...], values)).astype(BF16)
    attention = dot(mixture, proj_ref[...]).astype(BF16)

    middle = (x + attention.astype(F32)).astype(BF16)
    widened = middle.astype(F32)
    normal_two, inverse_two = norm_stats(widened)
    normed_two = (normal_two * gain_two).astype(BF16)
    cot = cot_ref[...]
    up_proj = dot(normed_two, up_ref[...])
    cumulative = 0.5 * (1.0 + lax.erf(up_proj * 0.7071067811865476))
    density = jnp.exp(-0.5 * up_proj * up_proj) * 0.3989422804014327
    active = (up_proj * cumulative).astype(BF16)
    out_ref[...] = (widened + dot_nt(active, down_ref[...])).astype(BF16)
    grad_down = dot_tn(cot, active).astype(BF16)
    delta_act = dot(cot, down_ref[...])
    delta_up = (delta_act * (cumulative + up_proj * density)).astype(BF16)
    grad_up = dot_tn(normed_two, delta_up).astype(BF16)
    for t in range(6):
        grads_ref[C * t : C * (t + 1)] = grad_up[:, LANES * t : LANES * (t + 1)]
        grads_ref[C * (t + 6) : C * (t + 7)] = grad_down[:, LANES * t : LANES * (t + 1)]
    delta_hidden = dot_nt(delta_up, up_ref[...])
    delta_input, grad_gain_two = norm_back(delta_hidden, normal_two, inverse_two, gain_two)
    delta_middle = (cot.astype(F32) + delta_input).astype(BF16)

    grad_proj = dot_tn(mixture, delta_middle)
    mixture_by = by_head(dot_nt(delta_middle, proj_ref[...]).astype(BF16))
    delta_value = dot_tn(low_ref[...], mixture_by)
    scores_ref[...] = dot_nt(mixture_by, values)
    for h in range(HEADS):
        at = pl.ds(h * WT, WT)
        prob = prob_ref[at, :]
        delta_prob = scores_ref[at, :]
        scores = prob * (delta_prob - jnp.sum(delta_prob * prob, axis=-1, keepdims=True))
        low_ref[at, :] = scores.astype(BF16)
        turned = scores[:, LANES:].T
        pairs_ref[h, :WT, :] = scores[:, :LANES]
        pairs_ref[h, WT : WT + TAIL, :] = turned[:, :LANES]
        pairs_ref[h, WT + TAIL :, :] = jnp.zeros((TAIL, LANES), F32)
        pairs_ref[h, WT + TAIL :, :TAIL] = turned[:, LANES:]
    delta_query = joined(dot(low_ref[...], keys)) * factor
    delta_key = dot_tn(low_ref[...], queries_by) * factor
    delta_packed = jnp.concatenate((delta_query, delta_key, delta_value), axis=1).astype(BF16)
    delta_normed = dot_nt(delta_packed, qkv_ref[...])
    grad_qkv = dot_tn(normed, delta_packed)
    for t in range(4):
        grads_ref[C * (t + 12) : C * (t + 13)] = grad_qkv[:, LANES * t : LANES * (t + 1)].astype(BF16)
    grads_ref[C * 16 : C * 17] = grad_proj[:, :LANES].astype(BF16)
    grads_ref[C * 17 : C * 18] = jnp.concatenate((grad_qkv[:, 4 * LANES :], grad_proj[:, LANES:]), axis=1).astype(BF16)
    delta_normed = delta_normed.astype(BF16).astype(F32)
    delta_input, grad_gain_one = norm_back(delta_normed, normal_one, inverse_one, gain_one)
    delta_ref[...] = (delta_middle.astype(F32) + delta_input).astype(BF16)
    gains = jnp.concatenate((grad_gain_one, grad_gain_two), axis=0)
    wide = jnp.concatenate((gains, jnp.zeros((2, 2 * LANES - C), F32)), axis=1)
    grads_ref[C * 18 :] = jnp.concatenate(
        (wide[:, :LANES], wide[:, LANES:], jnp.zeros((124, LANES), F32)), axis=0
    ).astype(BF16)


def block(*args):
    shapes = [
        ((WT, C), BF16),
        ((WT, C), BF16),
        ((GROWS, LANES), BF16),
        ((HEADS, ROWS, LANES), F32),
    ]
    return pl.pallas_call(
        block_kernel,
        out_shape=[jax.ShapeDtypeStruct(s, d) for s, d in shapes],
        scratch_shapes=[
            pltpu.VMEM((HEADS * WT, WT), F32),
            pltpu.VMEM((HEADS * WT, WT), F32),
            pltpu.VMEM((HEADS * WT, WT), BF16),
        ],
        name="block",
        compiler_params=pltpu.CompilerParams(vmem_limit_bytes=24 * 1024 * 1024),
        cost_estimate=pl.CostEstimate(flops=900_000_000, bytes_accessed=4_000_000, transcendentals=300_000),
    )(*args)


def unpack_kernel(grads_ref, *refs):
    outs, held, sems = refs[:6], refs[6:12], refs[12]
    gain_one_ref, gain_two_ref, qkv_ref, proj_ref, up_ref, down_ref = held
    factor = TOKENS ** (-0.5)
    copies = [pltpu.make_async_copy(held[k], outs[k], sems.at[k]) for k in range(6)]

    def rows(start, count):
        return grads_ref[start : start + count].astype(F32) * factor

    for t in range(6):
        up_ref[:, LANES * t : LANES * (t + 1)] = rows(C * t, C)
    copies[4].start()
    for t in range(6):
        down_ref[:, LANES * t : LANES * (t + 1)] = rows(C * (t + 6), C)
    copies[5].start()
    halves = rows(C * 17, C)
    for t in range(4):
        qkv_ref[:, LANES * t : LANES * (t + 1)] = rows(C * (t + 12), C)
    qkv_ref[:, 4 * LANES :] = halves[:, :64]
    copies[2].start()
    proj_ref[:, :LANES] = rows(C * 16, C)
    proj_ref[:, LANES:] = halves[:, 64:]
    copies[3].start()
    gains = rows(C * 18, 16)
    for k, ref in enumerate((gain_one_ref, gain_two_ref)):
        ref[...] = jnp.concatenate((gains[k : k + 1], gains[k + 2 : k + 3, : C - LANES]), axis=1)
        copies[k].start()
    for copy in copies:
        copy.wait()


def unpack(grads):
    shapes = [(1, C), (1, C), (C, 3 * C), (C, C), (C, HID), (C, HID)]
    return pl.pallas_call(
        unpack_kernel,
        out_shape=[jax.ShapeDtypeStruct(s, F32) for s in shapes],
        in_specs=[pl.BlockSpec(memory_space=pltpu.VMEM)],
        out_specs=[pl.BlockSpec(memory_space=pl.ANY)] * 6,
        scratch_shapes=[pltpu.VMEM(s, F32) for s in shapes] + [pltpu.SemaphoreType.DMA((6,))],
        name="unpack",
        compiler_params=pltpu.CompilerParams(vmem_limit_bytes=16 * 1024 * 1024),
        cost_estimate=pl.CostEstimate(flops=500_000, bytes_accessed=2_700_000, transcendentals=0),
    )(grads)


def neighbours(by):
    lat, lon = lax.axis_size("lat"), lax.axis_size("lon")
    return [
        (i * lon + j, (i + by) % lat * lon + (j + by) % lon) for i in range(lat) for j in range(lon)
    ]


def ring(axis, by):
    peers = lax.axis_size(axis)
    return [(i, (i + by) % peers) for i in range(peers)]


def shift_in(grid):
    from_lat = lax.ppermute(grid[:, :, :3, 6:], "lat", ring("lat", -1))
    from_lon = lax.ppermute(grid[:, :, 3:, :6], "lon", ring("lon", -1))
    from_both = lax.ppermute(grid[:, :, :3, :6], ("lat", "lon"), neighbours(-1))
    top = jnp.concatenate((grid[:, :, 3:, 6:], from_lon), axis=3)
    low = jnp.concatenate((from_lat, from_both), axis=3)
    return jnp.concatenate((top, low), axis=2)


def spread_over(axis, groups=None):
    return lambda parts: lax.all_to_all(parts, axis, 0, 0, axis_index_groups=groups)


def total(parts):
    return jnp.sum(parts.astype(F32), axis=0).astype(BF16)


def finish(grid, grads, pairs, pos_flat):
    lat, lon = lax.axis_size("lat"), lax.axis_size("lon")
    low, far = 2, 4
    high = lon // (low * far)
    place = lambda h, l, f: (h * low + l) * far + f
    over_low = spread_over(
        ("lat", "lon"),
        [[i * lon + place(h, l, f) for i in range(lat) for l in range(low)] for h in range(high) for f in range(far)],
    )
    over_high = spread_over("lon", [[place(h, l, f) for h in range(high)] for l in range(low) for f in range(far)])
    over_far = spread_over("lon", [[place(h, l, f) for f in range(far)] for h in range(high) for l in range(low)])
    other = [(j, j ^ far) for j in range(lon)]

    def same(part, count):
        return jnp.broadcast_to(part[None], (count,) + part.shape)

    share = GROWS // (lat * low)
    mine = total(over_low(grads.reshape(lat * low, share, LANES)))
    own = bias_grad(pairs, pos_flat).reshape(low, BROWS // low, LANES)
    at = lax.axis_index("lon") // far % low
    kept = lax.dynamic_index_in_dim(own, at, 0, keepdims=False)
    given = lax.dynamic_index_in_dim(own, 1 - at, 0, keepdims=False)
    bias = total(jnp.stack((kept, lax.ppermute(given, "lon", other))))
    both = jnp.concatenate((mine, bias), axis=0)
    rows_got = lax.ppermute(grid[:, :, 3:], "lat", ring("lat", 1))
    both = total(over_high(same(both, high)))
    both, rows_got = lax.optimization_barrier((both, rows_got))
    grid = jnp.concatenate((rows_got, grid[:, :, :3]), axis=2)
    cols_got = lax.ppermute(grid[:, :, :, 6:], "lon", ring("lon", 1))
    both = total(over_far(same(both, far)))
    both, cols_got = lax.optimization_barrier((both, cols_got))
    grid = jnp.concatenate((cols_got, grid[:, :, :, :6]), axis=3)
    grads = over_low(same(both[:share], lat * low)).reshape(GROWS, LANES)
    kept = both[share:]
    given = lax.ppermute(kept, "lon", other)
    first, second = jnp.where(at == 0, kept, given), jnp.where(at == 0, given, kept)
    return grid, grads, jnp.concatenate((first, second), axis=0).astype(F32)


def local(
    tokens,
    gain_one,
    gain_two,
    qkv_weight,
    proj_weight,
    up_weight,
    down_weight,
    bias_table,
    pos_index,
    mask_ids,
    cotangent,
):
    grid = tokens.shape
    moved = shift_in(jnp.stack((tokens, cotangent)))
    bias, pos_flat = bias_pairs(bias_table.reshape(HEADS, 1, NPOS), pos_index, mask_ids[::-1].reshape(1, WT))
    out, delta, grads, pairs = block(
        moved[0].reshape(WT, C),
        moved[1].reshape(WT, C),
        jnp.stack((gain_one, gain_two)),
        qkv_weight,
        proj_weight,
        up_weight,
        down_weight.T,
        bias,
    )
    back, grads, grad_bias = finish(jnp.stack((out, delta)).reshape((2,) + grid), grads, pairs, pos_flat)
    totals = unpack(grads)
    grad_bias = grad_bias[: HEADS * SLOTS].reshape(HEADS, SLOTS * LANES)[:, :NPOS]
    return (
        back[0],
        back[1],
        totals[0].reshape(C),
        totals[1].reshape(C),
        *totals[2:5],
        totals[5].T,
        grad_bias.reshape(HEADS, 1, 1, NPOS),
    )


def solution(mesh):
    in_specs = (
        P(None, "lat", "lon", None),
        P(),
        P(),
        P(),
        P(),
        P(),
        P(),
        P(None, None, "lat", None),
        P(),
        P(None, "lat", "lon"),
        P(None, "lat", "lon", None),
    )
    out_specs = (
        P(None, "lat", "lon", None),
        P(None, "lat", "lon", None),
        P(),
        P(),
        P(),
        P(),
        P(),
        P(),
        P(None, None, "lat", None),
    )
    return jax.shard_map(local, mesh=mesh, in_specs=in_specs, out_specs=out_specs, check_vma=False)
```

```python
import jax
import jax.numpy as jnp
from jax import lax
from jax.experimental import pallas as pl
from jax.experimental.pallas import tpu as pltpu
from jax.sharding import PartitionSpec as P

HEADS = 6
WT = 144
NPOS = 3312
C = 192
HID = 768
HEAD = C // HEADS
SLOTS = 26
LANES = 128
TOKENS = 73728
TAIL = WT - LANES
ROWS = WT + 2 * TAIL
GROWS = 3584
STEP = 44
BROWS = 160
LOW = 2
FAR = 4
EPS = 1e-05
F32 = jnp.float32
BF16 = jnp.bfloat16


def dot(a, b):
    return lax.dot_general(a, b, (((1,), (0,)), ((), ())), preferred_element_type=F32)


def dot_nt(a, b):
    return lax.dot_general(a, b, (((1,), (1,)), ((), ())), preferred_element_type=F32)


def dot_tn(a, b):
    return lax.dot_general(a, b, (((0,), (0,)), ((), ())), preferred_element_type=F32)


def norm_stats(widened):
    center = widened - jnp.mean(widened, axis=-1, keepdims=True)
    spread = jnp.mean(center * center, axis=-1, keepdims=True)
    inverse = lax.rsqrt(spread + EPS)
    return center * inverse, inverse


def norm_back(delta_hidden, normal, inverse, gain):
    grad_gain = jnp.sum(delta_hidden * normal, axis=0, keepdims=True)
    delta_normal = delta_hidden * gain
    delta_input = inverse * (
        delta_normal
        - jnp.mean(delta_normal, axis=-1, keepdims=True)
        - normal * jnp.mean(delta_normal * normal, axis=-1, keepdims=True)
    )
    return delta_input, grad_gain


def gather_kernel(table_ref, pos_ref, mask_ref, bias_ref, flat_pos_ref, slots_ref, flat_ref):
    half = WT // 2
    pos = pos_ref[...]
    pos = jnp.concatenate((pos[half:], pos[:half]), axis=0)
    pos = jnp.concatenate((pos[:, half:], pos[:, :half]), axis=1)
    turned = pos[:, LANES:].T
    flat_pos_ref[:WT] = pos[:, :LANES]
    flat_pos_ref[WT : WT + TAIL] = turned[:, :LANES]
    flat_pos_ref[WT + TAIL :] = jnp.zeros((TAIL, LANES), jnp.int32)
    flat_pos_ref[WT + TAIL :, :TAIL] = turned[:, LANES:]
    for h in range(HEADS):
        for g in range(SLOTS):
            count = min(LANES, NPOS - g * LANES)
            row = table_ref[h, :, g * LANES : g * LANES + count]
            slots_ref[h, g, :, :count] = jnp.broadcast_to(row, (8, count))

    def rows(i, carry):
        ats = [pl.ds(pl.multiple_of(i * 16 + 8 * k, 8), 8) for k in range(2)]
        pos = [flat_pos_ref[at, :] for at in ats]
        lane = [jnp.bitwise_and(p, LANES - 1) for p in pos]
        slot = [jnp.right_shift(p, 7) for p in pos]
        held = [[jnp.zeros((8, LANES), F32)] * HEADS for _ in ats]
        for g in range(SLOTS):
            here = [s == g for s in slot]
            for h in range(HEADS):
                row = slots_ref[h, g]
                for k in range(2):
                    got = jnp.take_along_axis(row, lane[k], axis=1)
                    held[k][h] = jnp.where(here[k], got, held[k][h])
        for k, at in enumerate(ats):
            for h in range(HEADS):
                flat_ref[h, at, :] = held[k][h]
        return carry

    lax.fori_loop(0, ROWS // 16, rows, 0)
    mask = jnp.broadcast_to(mask_ref[...], (WT, WT))
    allowed = mask == mask.T
    for h in range(HEADS):
        tail = jnp.concatenate((flat_ref[h, WT : WT + TAIL, :].T, flat_ref[h, WT + TAIL :, :].T[:TAIL]), axis=0)
        at = pl.ds(h * WT, WT)
        bias_ref[at, :LANES] = jnp.where(allowed[:, :LANES], flat_ref[h, :WT, :], -1e30)
        bias_ref[at, LANES:] = jnp.where(allowed[:, LANES:], tail, -1e30)


def bias_pairs(table, pos_index, mask_row):
    return pl.pallas_call(
        gather_kernel,
        out_shape=[jax.ShapeDtypeStruct((HEADS * WT, WT), F32), jax.ShapeDtypeStruct((ROWS, LANES), jnp.int32)],
        scratch_shapes=[pltpu.VMEM((HEADS, SLOTS, 8, LANES), F32), pltpu.VMEM((HEADS, ROWS, LANES), F32)],
        name="bias_pairs",
        compiler_params=pltpu.CompilerParams(vmem_limit_bytes=16 * 1024 * 1024),
        cost_estimate=pl.CostEstimate(flops=10_000_000, bytes_accessed=1_200_000, transcendentals=0),
    )(table, pos_index, mask_row)


def scatter_kernel(pairs_ref, pos_ref, out_ref, sums_ref, packed_ref):
    sums_ref[...] = jnp.zeros_like(sums_ref)
    slot_ids = lax.broadcasted_iota(jnp.int32, (32, LANES), 0)
    lane_ids = lax.broadcasted_iota(jnp.int32, (LANES, LANES), 0)

    def rows(i, carry):
        spread, onehot = [], []
        for j in range(STEP):
            at = pl.ds(i * STEP + j, 1)
            pos = pos_ref[at, :]
            slot = jnp.where(slot_ids == jnp.right_shift(pos, 7), 1.0, 0.0).astype(BF16)
            lane = jnp.bitwise_and(pos, LANES - 1)
            onehot.append(jnp.where(lane_ids == lane, 1.0, 0.0).astype(BF16))
            spread.append(
                jnp.concatenate(
                    [slot * jnp.broadcast_to(pairs_ref[h, at, :], (32, LANES)).astype(BF16) for h in range(HEADS)],
                    axis=0,
                )
            )
        sums_ref[...] += dot_nt(jnp.concatenate(spread, axis=1), jnp.concatenate(onehot, axis=1))
        return carry

    lax.fori_loop(0, ROWS // STEP, rows, 0)
    packed_ref[...] = jnp.zeros_like(packed_ref)
    for h in range(HEADS):
        packed_ref[h * SLOTS : (h + 1) * SLOTS] = sums_ref[h * 32 : h * 32 + SLOTS]
    out_ref[...] = packed_ref[...].astype(BF16)


def bias_grad(pairs, pos_flat):
    return pl.pallas_call(
        scatter_kernel,
        out_shape=jax.ShapeDtypeStruct((BROWS, LANES), BF16),
        scratch_shapes=[pltpu.VMEM((HEADS * 32, LANES), F32), pltpu.VMEM((BROWS, LANES), F32)],
        name="bias_grad",
        compiler_params=pltpu.CompilerParams(vmem_limit_bytes=16 * 1024 * 1024),
        cost_estimate=pl.CostEstimate(flops=1_100_000_000, bytes_accessed=700_000, transcendentals=0),
    )(pairs, pos_flat)


def block_kernel(
    x_ref,
    cot_ref,
    gain_one_ref,
    gain_two_ref,
    qkv_ref,
    proj_ref,
    up_ref,
    down_ref,
    bias_ref,
    out_ref,
    delta_ref,
    grads_ref,
    pairs_ref,
    scores_ref,
    prob_ref,
    low_ref,
):
    factor = HEAD ** (-0.5)
    x = x_ref[...].astype(F32)
    gain_one = gain_one_ref[...]
    gain_two = gain_two_ref[...]
    normal_one, inverse_one = norm_stats(x)
    normed = (normal_one * gain_one).astype(BF16)
    packed = dot(normed, qkv_ref[...]).astype(BF16)
    queries, keys, values = packed[:, :C], packed[:, C : 2 * C], packed[:, 2 * C :]
    head_of = lax.broadcasted_iota(jnp.int32, (WT, C), 1) // HEAD

    def by_head(a):
        return jnp.concatenate([jnp.where(head_of == h, a, jnp.zeros_like(a)) for h in range(HEADS)], axis=0)

    def joined(a):
        out = a[:WT]
        for h in range(1, HEADS):
            out = jnp.where(head_of == h, a[h * WT : (h + 1) * WT], out)
        return out

    queries_by = by_head(queries)
    scores_ref[...] = dot_nt(queries_by, keys)
    for h in range(HEADS):
        at = pl.ds(h * WT, WT)
        scores = scores_ref[at, :] * factor + bias_ref[at, :]
        weight = jnp.exp(scores - jnp.max(scores, axis=-1, keepdims=True))
        prob = weight * (1.0 / jnp.sum(weight, axis=-1, keepdims=True))
        prob_ref[at, :] = prob
        low_ref[at, :] = prob.astype(BF16)
    mixture = joined(dot(low_ref[...], values)).astype(BF16)
    attention = dot(mixture, proj_ref[...]).astype(BF16)

    middle = (x + attention.astype(F32)).astype(BF16)
    widened = middle.astype(F32)
    normal_two, inverse_two = norm_stats(widened)
    normed_two = (normal_two * gain_two).astype(BF16)
    cot = cot_ref[...]
    up_proj = dot(normed_two, up_ref[...])
    cumulative = 0.5 * (1.0 + lax.erf(up_proj * 0.7071067811865476))
    density = jnp.exp(-0.5 * up_proj * up_proj) * 0.3989422804014327
    active = (up_proj * cumulative).astype(BF16)
    out_ref[...] = (widened + dot_nt(active, down_ref[...])).astype(BF16)
    grad_down = dot_tn(cot, active).astype(BF16)
    delta_act = dot(cot, down_ref[...])
    delta_up = (delta_act * (cumulative + up_proj * density)).astype(BF16)
    grad_up = dot_tn(normed_two, delta_up).astype(BF16)
    for t in range(6):
        grads_ref[C * t : C * (t + 1)] = grad_up[:, LANES * t : LANES * (t + 1)]
        grads_ref[C * (t + 6) : C * (t + 7)] = grad_down[:, LANES * t : LANES * (t + 1)]
    delta_hidden = dot_nt(delta_up, up_ref[...])
    delta_input, grad_gain_two = norm_back(delta_hidden, normal_two, inverse_two, gain_two)
    delta_middle = (cot.astype(F32) + delta_input).astype(BF16)

    grad_proj = dot_tn(mixture, delta_middle)
    mixture_by = by_head(dot_nt(delta_middle, proj_ref[...]).astype(BF16))
    delta_value = dot_tn(low_ref[...], mixture_by)
    scores_ref[...] = dot_nt(mixture_by, values)
    for h in range(HEADS):
        at = pl.ds(h * WT, WT)
        prob = prob_ref[at, :]
        delta_prob = scores_ref[at, :]
        scores = prob * (delta_prob - jnp.sum(delta_prob * prob, axis=-1, keepdims=True))
        low_ref[at, :] = scores.astype(BF16)
        turned = scores[:, LANES:].T
        pairs_ref[h, :WT, :] = scores[:, :LANES]
        pairs_ref[h, WT : WT + TAIL, :] = turned[:, :LANES]
        pairs_ref[h, WT + TAIL :, :] = jnp.zeros((TAIL, LANES), F32)
        pairs_ref[h, WT + TAIL :, :TAIL] = turned[:, LANES:]
    delta_query = joined(dot(low_ref[...], keys)) * factor
    delta_key = dot_tn(low_ref[...], queries_by) * factor
    delta_packed = jnp.concatenate((delta_query, delta_key, delta_value), axis=1).astype(BF16)
    delta_normed = dot_nt(delta_packed, qkv_ref[...])
    grad_qkv = dot_tn(normed, delta_packed)
    for t in range(4):
        grads_ref[C * (t + 12) : C * (t + 13)] = grad_qkv[:, LANES * t : LANES * (t + 1)].astype(BF16)
    grads_ref[C * 16 : C * 17] = grad_proj[:, :LANES].astype(BF16)
    grads_ref[C * 17 : C * 18] = jnp.concatenate((grad_qkv[:, 4 * LANES :], grad_proj[:, LANES:]), axis=1).astype(BF16)
    delta_normed = delta_normed.astype(BF16).astype(F32)
    delta_input, grad_gain_one = norm_back(delta_normed, normal_one, inverse_one, gain_one)
    delta_ref[...] = (delta_middle.astype(F32) + delta_input).astype(BF16)
    gains = jnp.concatenate((grad_gain_one, grad_gain_two), axis=0)
    wide = jnp.concatenate((gains, jnp.zeros((2, 2 * LANES - C), F32)), axis=1)
    grads_ref[C * 18 :] = jnp.concatenate(
        (wide[:, :LANES], wide[:, LANES:], jnp.zeros((124, LANES), F32)), axis=0
    ).astype(BF16)


def block(*args):
    shapes = [
        ((WT, C), BF16),
        ((WT, C), BF16),
        ((GROWS, LANES), BF16),
        ((HEADS, ROWS, LANES), F32),
    ]
    return pl.pallas_call(
        block_kernel,
        out_shape=[jax.ShapeDtypeStruct(s, d) for s, d in shapes],
        scratch_shapes=[
            pltpu.VMEM((HEADS * WT, WT), F32),
            pltpu.VMEM((HEADS * WT, WT), F32),
            pltpu.VMEM((HEADS * WT, WT), BF16),
        ],
        name="block",
        compiler_params=pltpu.CompilerParams(vmem_limit_bytes=24 * 1024 * 1024),
        cost_estimate=pl.CostEstimate(flops=900_000_000, bytes_accessed=4_000_000, transcendentals=300_000),
    )(*args)


def unpack_kernel(
    grads_ref, kept_ref, given_ref, gain_one_ref, gain_two_ref, qkv_ref, proj_ref, up_ref, down_ref, bias_ref
):
    factor = TOKENS ** (-0.5)

    def rows(start, count):
        return grads_ref[start : start + count].astype(F32) * factor

    for t in range(6):
        at = slice(LANES * t, LANES * (t + 1))
        up_ref[:, at] = rows(C * t, C)
        down_ref[:, at] = rows(C * (t + 6), C)
        if t < 4:
            qkv_ref[:, at] = rows(C * (t + 12), C)
    halves = rows(C * 17, C)
    qkv_ref[:, 4 * LANES :] = halves[:, :64]
    proj_ref[:, :LANES] = rows(C * 16, C)
    proj_ref[:, LANES:] = halves[:, 64:]
    gains = rows(C * 18, 16)
    for k, ref in enumerate((gain_one_ref, gain_two_ref)):
        ref[...] = jnp.concatenate((gains[k : k + 1], gains[k + 2 : k + 3, : C - LANES]), axis=1)
    first = lax.axis_index("lon") // FAR % LOW == 0
    kept, given = kept_ref[...].astype(F32), given_ref[...].astype(F32)
    sums = (jnp.where(first, kept, given), jnp.where(first, given, kept))
    for h in range(HEADS):
        for g in range(SLOTS):
            half, row = divmod(h * SLOTS + g, BROWS // LOW)
            count = min(LANES, NPOS - g * LANES)
            bias_ref[h, :, g * LANES : g * LANES + count] = sums[half][row : row + 1, :count]


def unpack(grads, kept, given):
    shapes = [(1, C), (1, C), (C, 3 * C), (C, C), (C, HID), (C, HID), (HEADS, 1, NPOS)]
    return pl.pallas_call(
        unpack_kernel,
        out_shape=[jax.ShapeDtypeStruct(s, F32) for s in shapes],
        name="unpack",
        compiler_params=pltpu.CompilerParams(vmem_limit_bytes=16 * 1024 * 1024),
        cost_estimate=pl.CostEstimate(flops=500_000, bytes_accessed=2_700_000, transcendentals=0),
    )(grads, kept, given)


def neighbours(by):
    lat, lon = lax.axis_size("lat"), lax.axis_size("lon")
    return [
        (i * lon + j, (i + by) % lat * lon + (j + by) % lon) for i in range(lat) for j in range(lon)
    ]


def ring(axis, by):
    peers = lax.axis_size(axis)
    return [(i, (i + by) % peers) for i in range(peers)]


def shift_in(grid):
    from_lat = lax.ppermute(grid[:, :, :3, 6:], "lat", ring("lat", -1))
    from_lon = lax.ppermute(grid[:, :, 3:, :6], "lon", ring("lon", -1))
    from_both = lax.ppermute(grid[:, :, :3, :6], ("lat", "lon"), neighbours(-1))
    top = jnp.concatenate((grid[:, :, 3:, 6:], from_lon), axis=3)
    low = jnp.concatenate((from_lat, from_both), axis=3)
    return jnp.concatenate((top, low), axis=2)


def spread_over(axis, groups=None):
    return lambda parts: lax.all_to_all(parts, axis, 0, 0, axis_index_groups=groups)


def total(parts):
    return jnp.sum(parts.astype(F32), axis=0).astype(BF16)


def finish(grid, grads, pairs, pos_flat):
    lat, lon = lax.axis_size("lat"), lax.axis_size("lon")
    low, far = LOW, FAR
    high = lon // (low * far)
    place = lambda h, l, f: (h * low + l) * far + f
    over_low = spread_over(
        ("lat", "lon"),
        [[i * lon + place(h, l, f) for i in range(lat) for l in range(low)] for h in range(high) for f in range(far)],
    )
    over_high = spread_over("lon", [[place(h, l, f) for h in range(high)] for l in range(low) for f in range(far)])
    over_far = spread_over("lon", [[place(h, l, f) for f in range(far)] for h in range(high) for l in range(low)])
    other = [(j, j ^ far) for j in range(lon)]

    def same(part, count):
        return jnp.broadcast_to(part[None], (count,) + part.shape)

    share = GROWS // (lat * low)
    mine = total(over_low(grads.reshape(lat * low, share, LANES)))
    own = bias_grad(pairs, pos_flat).reshape(low, BROWS // low, LANES)
    at = lax.axis_index("lon") // far % low
    kept = lax.dynamic_index_in_dim(own, at, 0, keepdims=False)
    given = lax.dynamic_index_in_dim(own, 1 - at, 0, keepdims=False)
    bias = total(jnp.stack((kept, lax.ppermute(given, "lon", other))))
    both = jnp.concatenate((mine, bias), axis=0)
    rows_got = lax.ppermute(grid[:, :, 3:], "lat", ring("lat", 1))
    both, rows_got = lax.optimization_barrier((both, rows_got))
    grid = jnp.concatenate((rows_got, grid[:, :, :3]), axis=2)
    cols_got = lax.ppermute(grid[:, :, :, 6:], "lon", ring("lon", 1))
    both = total(over_high(same(both, high)))
    both, cols_got = lax.optimization_barrier((both, cols_got))
    both = total(over_far(same(both, far)))
    grid = jnp.concatenate((cols_got, grid[:, :, :, :6]), axis=3)
    grads = over_low(same(both[:share], lat * low)).reshape(GROWS, LANES)
    kept = both[share:]
    given = lax.ppermute(kept, "lon", other)
    return grid, grads, kept, given


def local(
    tokens,
    gain_one,
    gain_two,
    qkv_weight,
    proj_weight,
    up_weight,
    down_weight,
    bias_table,
    pos_index,
    mask_ids,
    cotangent,
):
    grid = tokens.shape
    moved = shift_in(jnp.stack((tokens, cotangent)))
    bias, pos_flat = bias_pairs(bias_table.reshape(HEADS, 1, NPOS), pos_index, mask_ids[::-1].reshape(1, WT))
    out, delta, grads, pairs = block(
        moved[0].reshape(WT, C),
        moved[1].reshape(WT, C),
        gain_one.reshape(1, C),
        gain_two.reshape(1, C),
        qkv_weight,
        proj_weight,
        up_weight,
        down_weight.T,
        bias,
    )
    back, grads, kept, given = finish(jnp.stack((out, delta)).reshape((2,) + grid), grads, pairs, pos_flat)
    totals = unpack(grads, kept, given)
    return (
        back[0],
        back[1],
        totals[0].reshape(C),
        totals[1].reshape(C),
        *totals[2:5],
        totals[5].T,
        totals[6].reshape(HEADS, 1, 1, NPOS),
    )


def solution(mesh):
    in_specs = (
        P(None, "lat", "lon", None),
        P(),
        P(),
        P(),
        P(),
        P(),
        P(),
        P(None, None, "lat", None),
        P(),
        P(None, "lat", "lon"),
        P(None, "lat", "lon", None),
    )
    out_specs = (
        P(None, "lat", "lon", None),
        P(None, "lat", "lon", None),
        P(),
        P(),
        P(),
        P(),
        P(),
        P(),
        P(None, None, "lat", None),
    )
    return jax.shard_map(local, mesh=mesh, in_specs=in_specs, out_specs=out_specs, check_vma=False)
```

```python
import jax
import jax.numpy as jnp
from jax import lax
from jax.experimental import pallas as pl
from jax.experimental.pallas import tpu as pltpu
from jax.sharding import PartitionSpec as P

HEADS = 6
WT = 144
NPOS = 3312
C = 192
HID = 768
HEAD = C // HEADS
SLOTS = 26
LANES = 128
TOKENS = 73728
TAIL = WT - LANES
ROWS = WT + 2 * TAIL
GROWS = 3584
STEP = 44
BROWS = 160
LOW = 2
FAR = 4
EPS = 1e-05
F32 = jnp.float32
BF16 = jnp.bfloat16


def dot(a, b):
    return lax.dot_general(a, b, (((1,), (0,)), ((), ())), preferred_element_type=F32)


def dot_nt(a, b):
    return lax.dot_general(a, b, (((1,), (1,)), ((), ())), preferred_element_type=F32)


def dot_tn(a, b):
    return lax.dot_general(a, b, (((0,), (0,)), ((), ())), preferred_element_type=F32)


def norm_stats(widened):
    center = widened - jnp.mean(widened, axis=-1, keepdims=True)
    spread = jnp.mean(center * center, axis=-1, keepdims=True)
    inverse = lax.rsqrt(spread + EPS)
    return center * inverse, inverse


def norm_back(delta_hidden, normal, inverse, gain):
    grad_gain = jnp.sum(delta_hidden * normal, axis=0, keepdims=True)
    delta_normal = delta_hidden * gain
    delta_input = inverse * (
        delta_normal
        - jnp.mean(delta_normal, axis=-1, keepdims=True)
        - normal * jnp.mean(delta_normal * normal, axis=-1, keepdims=True)
    )
    return delta_input, grad_gain


def gather_kernel(table_ref, pos_ref, mask_ref, bias_ref, flat_pos_ref, slots_ref, flat_ref):
    half = WT // 2
    pos = pos_ref[...]
    pos = jnp.concatenate((pos[half:], pos[:half]), axis=0)
    pos = jnp.concatenate((pos[:, half:], pos[:, :half]), axis=1)
    turned = pos[:, LANES:].T
    flat_pos_ref[:WT] = pos[:, :LANES]
    flat_pos_ref[WT : WT + TAIL] = turned[:, :LANES]
    flat_pos_ref[WT + TAIL :] = jnp.zeros((TAIL, LANES), jnp.int32)
    flat_pos_ref[WT + TAIL :, :TAIL] = turned[:, LANES:]
    for h in range(HEADS):
        for g in range(SLOTS):
            count = min(LANES, NPOS - g * LANES)
            row = table_ref[h, :, g * LANES : g * LANES + count]
            slots_ref[h, g, :, :count] = jnp.broadcast_to(row, (8, count))

    def rows(i, carry):
        ats = [pl.ds(pl.multiple_of(i * 16 + 8 * k, 8), 8) for k in range(2)]
        pos = [flat_pos_ref[at, :] for at in ats]
        lane = [jnp.bitwise_and(p, LANES - 1) for p in pos]
        slot = [jnp.right_shift(p, 7) for p in pos]
        held = [[jnp.zeros((8, LANES), F32)] * HEADS for _ in ats]
        for g in range(SLOTS):
            here = [s == g for s in slot]
            for h in range(HEADS):
                row = slots_ref[h, g]
                for k in range(2):
                    got = jnp.take_along_axis(row, lane[k], axis=1)
                    held[k][h] = jnp.where(here[k], got, held[k][h])
        for k, at in enumerate(ats):
            for h in range(HEADS):
                flat_ref[h, at, :] = held[k][h]
        return carry

    lax.fori_loop(0, ROWS // 16, rows, 0)
    mask = jnp.broadcast_to(mask_ref[...], (WT, WT))
    allowed = mask == mask.T
    for h in range(HEADS):
        tail = jnp.concatenate((flat_ref[h, WT : WT + TAIL, :].T, flat_ref[h, WT + TAIL :, :].T[:TAIL]), axis=0)
        at = pl.ds(h * WT, WT)
        bias_ref[at, :LANES] = jnp.where(allowed[:, :LANES], flat_ref[h, :WT, :], -1e30)
        bias_ref[at, LANES:] = jnp.where(allowed[:, LANES:], tail, -1e30)


def bias_pairs(table, pos_index, mask_row):
    return pl.pallas_call(
        gather_kernel,
        out_shape=[jax.ShapeDtypeStruct((HEADS * WT, WT), F32), jax.ShapeDtypeStruct((ROWS, LANES), jnp.int32)],
        scratch_shapes=[pltpu.VMEM((HEADS, SLOTS, 8, LANES), F32), pltpu.VMEM((HEADS, ROWS, LANES), F32)],
        name="bias_pairs",
        compiler_params=pltpu.CompilerParams(vmem_limit_bytes=16 * 1024 * 1024),
        cost_estimate=pl.CostEstimate(flops=10_000_000, bytes_accessed=1_200_000, transcendentals=0),
    )(table, pos_index, mask_row)


def scatter_kernel(pairs_ref, pos_ref, out_ref, sums_ref, packed_ref):
    sums_ref[...] = jnp.zeros_like(sums_ref)
    slot_ids = lax.broadcasted_iota(jnp.int32, (32, LANES), 0)
    lane_ids = lax.broadcasted_iota(jnp.int32, (LANES, LANES), 0)

    def rows(i, carry):
        spread, onehot = [], []
        for j in range(STEP):
            at = pl.ds(i * STEP + j, 1)
            pos = pos_ref[at, :]
            slot = jnp.where(slot_ids == jnp.right_shift(pos, 7), 1.0, 0.0).astype(BF16)
            lane = jnp.bitwise_and(pos, LANES - 1)
            onehot.append(jnp.where(lane_ids == lane, 1.0, 0.0).astype(BF16))
            spread.append(
                jnp.concatenate(
                    [slot * jnp.broadcast_to(pairs_ref[h, at, :], (32, LANES)).astype(BF16) for h in range(HEADS)],
                    axis=0,
                )
            )
        sums_ref[...] += dot_nt(jnp.concatenate(spread, axis=1), jnp.concatenate(onehot, axis=1))
        return carry

    lax.fori_loop(0, ROWS // STEP, rows, 0)
    packed_ref[...] = jnp.zeros_like(packed_ref)
    for h in range(HEADS):
        packed_ref[h * SLOTS : (h + 1) * SLOTS] = sums_ref[h * 32 : h * 32 + SLOTS]
    out_ref[...] = packed_ref[...].astype(BF16)


def bias_grad(pairs, pos_flat):
    return pl.pallas_call(
        scatter_kernel,
        out_shape=jax.ShapeDtypeStruct((BROWS, LANES), BF16),
        scratch_shapes=[pltpu.VMEM((HEADS * 32, LANES), F32), pltpu.VMEM((BROWS, LANES), F32)],
        name="bias_grad",
        compiler_params=pltpu.CompilerParams(vmem_limit_bytes=16 * 1024 * 1024),
        cost_estimate=pl.CostEstimate(flops=1_100_000_000, bytes_accessed=700_000, transcendentals=0),
    )(pairs, pos_flat)


def block_kernel(
    x_ref,
    cot_ref,
    gain_one_ref,
    gain_two_ref,
    qkv_ref,
    proj_ref,
    up_ref,
    down_ref,
    bias_ref,
    out_ref,
    delta_ref,
    grads_ref,
    pairs_ref,
    scores_ref,
    prob_ref,
    low_ref,
):
    factor = HEAD ** (-0.5)
    x = x_ref[...].astype(F32)
    gain_one = gain_one_ref[...]
    gain_two = gain_two_ref[...]
    normal_one, inverse_one = norm_stats(x)
    normed = (normal_one * gain_one).astype(BF16)
    packed = dot(normed, qkv_ref[...]).astype(BF16)
    queries, keys, values = packed[:, :C], packed[:, C : 2 * C], packed[:, 2 * C :]
    head_of = lax.broadcasted_iota(jnp.int32, (WT, C), 1) // HEAD

    def by_head(a):
        return jnp.concatenate([jnp.where(head_of == h, a, jnp.zeros_like(a)) for h in range(HEADS)], axis=0)

    def joined(a):
        out = a[:WT]
        for h in range(1, HEADS):
            out = jnp.where(head_of == h, a[h * WT : (h + 1) * WT], out)
        return out

    queries_by = by_head(queries)
    scores_ref[...] = dot_nt(queries_by, keys)
    for h in range(HEADS):
        at = pl.ds(h * WT, WT)
        scores = scores_ref[at, :] * factor + bias_ref[at, :]
        weight = jnp.exp(scores - jnp.max(scores, axis=-1, keepdims=True))
        prob = weight * (1.0 / jnp.sum(weight, axis=-1, keepdims=True))
        prob_ref[at, :] = prob
        low_ref[at, :] = prob.astype(BF16)
    mixture = joined(dot(low_ref[...], values)).astype(BF16)
    attention = dot(mixture, proj_ref[...]).astype(BF16)

    middle = (x + attention.astype(F32)).astype(BF16)
    widened = middle.astype(F32)
    normal_two, inverse_two = norm_stats(widened)
    normed_two = (normal_two * gain_two).astype(BF16)
    cot = cot_ref[...]
    up_proj = dot(normed_two, up_ref[...])
    cumulative = 0.5 * (1.0 + lax.erf(up_proj * 0.7071067811865476))
    density = jnp.exp(-0.5 * up_proj * up_proj) * 0.3989422804014327
    active = (up_proj * cumulative).astype(BF16)
    out_ref[...] = (widened + dot_nt(active, down_ref[...])).astype(BF16)
    grad_down = dot_tn(cot, active).astype(BF16)
    delta_act = dot(cot, down_ref[...])
    delta_up = (delta_act * (cumulative + up_proj * density)).astype(BF16)
    grad_up = dot_tn(normed_two, delta_up).astype(BF16)
    for t in range(6):
        grads_ref[C * t : C * (t + 1)] = grad_up[:, LANES * t : LANES * (t + 1)]
        grads_ref[C * (t + 6) : C * (t + 7)] = grad_down[:, LANES * t : LANES * (t + 1)]
    delta_hidden = dot_nt(delta_up, up_ref[...])
    delta_input, grad_gain_two = norm_back(delta_hidden, normal_two, inverse_two, gain_two)
    delta_middle = (cot.astype(F32) + delta_input).astype(BF16)

    grad_proj = dot_tn(mixture, delta_middle)
    mixture_by = by_head(dot_nt(delta_middle, proj_ref[...]).astype(BF16))
    delta_value = dot_tn(low_ref[...], mixture_by)
    scores_ref[...] = dot_nt(mixture_by, values)
    for h in range(HEADS):
        at = pl.ds(h * WT, WT)
        prob = prob_ref[at, :]
        delta_prob = scores_ref[at, :]
        scores = prob * (delta_prob - jnp.sum(delta_prob * prob, axis=-1, keepdims=True))
        low_ref[at, :] = scores.astype(BF16)
        turned = scores[:, LANES:].T
        pairs_ref[h, :WT, :] = scores[:, :LANES]
        pairs_ref[h, WT : WT + TAIL, :] = turned[:, :LANES]
        pairs_ref[h, WT + TAIL :, :] = jnp.zeros((TAIL, LANES), F32)
        pairs_ref[h, WT + TAIL :, :TAIL] = turned[:, LANES:]
    delta_query = joined(dot(low_ref[...], keys)) * factor
    delta_key = dot_tn(low_ref[...], queries_by) * factor
    delta_packed = jnp.concatenate((delta_query, delta_key, delta_value), axis=1).astype(BF16)
    delta_normed = dot_nt(delta_packed, qkv_ref[...])
    grad_qkv = dot_tn(normed, delta_packed)
    for t in range(4):
        grads_ref[C * (t + 12) : C * (t + 13)] = grad_qkv[:, LANES * t : LANES * (t + 1)].astype(BF16)
    grads_ref[C * 16 : C * 17] = grad_proj[:, :LANES].astype(BF16)
    grads_ref[C * 17 : C * 18] = jnp.concatenate((grad_qkv[:, 4 * LANES :], grad_proj[:, LANES:]), axis=1).astype(BF16)
    delta_normed = delta_normed.astype(BF16).astype(F32)
    delta_input, grad_gain_one = norm_back(delta_normed, normal_one, inverse_one, gain_one)
    delta_ref[...] = (delta_middle.astype(F32) + delta_input).astype(BF16)
    gains = jnp.concatenate((grad_gain_one, grad_gain_two), axis=0)
    wide = jnp.concatenate((gains, jnp.zeros((2, 2 * LANES - C), F32)), axis=1)
    grads_ref[C * 18 :] = jnp.concatenate(
        (wide[:, :LANES], wide[:, LANES:], jnp.zeros((124, LANES), F32)), axis=0
    ).astype(BF16)


def block(*args):
    shapes = [
        ((WT, C), BF16),
        ((WT, C), BF16),
        ((GROWS, LANES), BF16),
        ((HEADS, ROWS, LANES), F32),
    ]
    return pl.pallas_call(
        block_kernel,
        out_shape=[jax.ShapeDtypeStruct(s, d) for s, d in shapes],
        scratch_shapes=[
            pltpu.VMEM((HEADS * WT, WT), F32),
            pltpu.VMEM((HEADS * WT, WT), F32),
            pltpu.VMEM((HEADS * WT, WT), BF16),
        ],
        name="block",
        compiler_params=pltpu.CompilerParams(vmem_limit_bytes=24 * 1024 * 1024),
        cost_estimate=pl.CostEstimate(flops=900_000_000, bytes_accessed=4_000_000, transcendentals=300_000),
    )(*args)


def unpack_kernel(
    grads_ref, kept_ref, given_ref, gain_one_ref, gain_two_ref, qkv_ref, proj_ref, up_ref, down_ref, bias_ref
):
    factor = TOKENS ** (-0.5)

    def rows(start, count):
        return grads_ref[start : start + count].astype(F32) * factor

    for t in range(6):
        at = slice(LANES * t, LANES * (t + 1))
        up_ref[:, at] = rows(C * t, C)
        down_ref[:, at] = rows(C * (t + 6), C)
        if t < 4:
            qkv_ref[:, at] = rows(C * (t + 12), C)
    halves = rows(C * 17, C)
    qkv_ref[:, 4 * LANES :] = halves[:, :64]
    proj_ref[:, :LANES] = rows(C * 16, C)
    proj_ref[:, LANES:] = halves[:, 64:]
    gains = rows(C * 18, 16)
    for k, ref in enumerate((gain_one_ref, gain_two_ref)):
        ref[...] = jnp.concatenate((gains[k : k + 1], gains[k + 2 : k + 3, : C - LANES]), axis=1)
    first = lax.axis_index("lon") // FAR % LOW == 0
    kept, given = kept_ref[...].astype(F32), given_ref[...].astype(F32)
    sums = (jnp.where(first, kept, given), jnp.where(first, given, kept))
    for h in range(HEADS):
        for g in range(SLOTS):
            half, row = divmod(h * SLOTS + g, BROWS // LOW)
            count = min(LANES, NPOS - g * LANES)
            bias_ref[h, :, g * LANES : g * LANES + count] = sums[half][row : row + 1, :count]


def unpack(grads, kept, given):
    shapes = [(1, C), (1, C), (C, 3 * C), (C, C), (C, HID), (C, HID), (HEADS, 1, NPOS)]
    return pl.pallas_call(
        unpack_kernel,
        out_shape=[jax.ShapeDtypeStruct(s, F32) for s in shapes],
        name="unpack",
        compiler_params=pltpu.CompilerParams(vmem_limit_bytes=16 * 1024 * 1024),
        cost_estimate=pl.CostEstimate(flops=500_000, bytes_accessed=2_700_000, transcendentals=0),
    )(grads, kept, given)


def neighbours(by):
    lat, lon = lax.axis_size("lat"), lax.axis_size("lon")
    return [
        (i * lon + j, (i + by) % lat * lon + (j + by) % lon) for i in range(lat) for j in range(lon)
    ]


def ring(axis, by):
    peers = lax.axis_size(axis)
    return [(i, (i + by) % peers) for i in range(peers)]


def shift_in(grid):
    def moved(piece, axis, pairs):
        return lax.ppermute(piece.reshape(-1, C), axis, pairs).reshape(piece.shape)

    from_lat = moved(grid[:, :, :3, 6:], "lat", ring("lat", -1))
    from_lon = moved(grid[:, :, 3:, :6], "lon", ring("lon", -1))
    from_both = moved(grid[:, :, :3, :6], ("lat", "lon"), neighbours(-1))
    top = jnp.concatenate((grid[:, :, 3:, 6:], from_lon), axis=3)
    low = jnp.concatenate((from_lat, from_both), axis=3)
    return jnp.concatenate((top, low), axis=2)


def flat_permute(piece, axis):
    return lax.ppermute(piece.reshape(-1, C), axis, ring(axis, 1)).reshape(piece.shape)


def spread_over(axis, groups=None):
    return lambda parts: lax.all_to_all(parts, axis, 0, 0, axis_index_groups=groups)


def total(parts):
    return jnp.sum(parts.astype(F32), axis=0).astype(BF16)


def finish(grid, grads, pairs, pos_flat):
    lat, lon = lax.axis_size("lat"), lax.axis_size("lon")
    low, far = LOW, FAR
    high = lon // (low * far)
    place = lambda h, l, f: (h * low + l) * far + f
    over_low = spread_over(
        ("lat", "lon"),
        [[i * lon + place(h, l, f) for i in range(lat) for l in range(low)] for h in range(high) for f in range(far)],
    )
    over_high = spread_over("lon", [[place(h, l, f) for h in range(high)] for l in range(low) for f in range(far)])
    over_far = spread_over("lon", [[place(h, l, f) for f in range(far)] for h in range(high) for l in range(low)])
    other = [(j, j ^ far) for j in range(lon)]

    def same(part, count):
        return jnp.broadcast_to(part[None], (count,) + part.shape)

    share = GROWS // (lat * low)
    mine = total(over_low(grads.reshape(lat * low, share, LANES)))
    own = bias_grad(pairs, pos_flat).reshape(low, BROWS // low, LANES)
    at = lax.axis_index("lon") // far % low
    kept = lax.dynamic_index_in_dim(own, at, 0, keepdims=False)
    given = lax.dynamic_index_in_dim(own, 1 - at, 0, keepdims=False)
    bias = total(jnp.stack((kept, lax.ppermute(given, "lon", other))))
    both = jnp.concatenate((mine, bias), axis=0)
    rows_got = flat_permute(grid[:, :, 3:], "lat")
    both, rows_got = lax.optimization_barrier((both, rows_got))
    grid = jnp.concatenate((rows_got, grid[:, :, :3]), axis=2)
    cols_got = flat_permute(grid[:, :, :, 6:], "lon")
    both = total(over_high(same(both, high)))
    both, cols_got = lax.optimization_barrier((both, cols_got))
    both = total(over_far(same(both, far)))
    grid = jnp.concatenate((cols_got, grid[:, :, :, :6]), axis=3)
    grads = over_low(same(both[:share], lat * low)).reshape(GROWS, LANES)
    kept = both[share:]
    given = lax.ppermute(kept, "lon", other)
    return grid, grads, kept, given


def local(
    tokens,
    gain_one,
    gain_two,
    qkv_weight,
    proj_weight,
    up_weight,
    down_weight,
    bias_table,
    pos_index,
    mask_ids,
    cotangent,
):
    grid = tokens.shape
    moved = shift_in(jnp.stack((tokens, cotangent)))
    bias, pos_flat = bias_pairs(bias_table.reshape(HEADS, 1, NPOS), pos_index, mask_ids[::-1].reshape(1, WT))
    out, delta, grads, pairs = block(
        moved[0].reshape(WT, C),
        moved[1].reshape(WT, C),
        gain_one.reshape(1, C),
        gain_two.reshape(1, C),
        qkv_weight,
        proj_weight,
        up_weight,
        down_weight.T,
        bias,
    )
    back, grads, kept, given = finish(jnp.stack((out, delta)).reshape((2,) + grid), grads, pairs, pos_flat)
    totals = unpack(grads, kept, given)
    return (
        back[0],
        back[1],
        totals[0].reshape(C),
        totals[1].reshape(C),
        *totals[2:5],
        totals[5].T,
        totals[6].reshape(HEADS, 1, 1, NPOS),
    )


def solution(mesh):
    in_specs = (
        P(None, "lat", "lon", None),
        P(),
        P(),
        P(),
        P(),
        P(),
        P(),
        P(None, None, "lat", None),
        P(),
        P(None, "lat", "lon"),
        P(None, "lat", "lon", None),
    )
    out_specs = (
        P(None, "lat", "lon", None),
        P(None, "lat", "lon", None),
        P(),
        P(),
        P(),
        P(),
        P(),
        P(),
        P(None, None, "lat", None),
    )
    return jax.shard_map(local, mesh=mesh, in_specs=in_specs, out_specs=out_specs, check_vma=False)
```

```python
import jax
import jax.numpy as jnp
from jax import lax
from jax.experimental import pallas as pl
from jax.experimental.pallas import tpu as pltpu
from jax.sharding import PartitionSpec as P

HEADS = 6
WT = 144
NPOS = 3312
C = 192
HID = 768
HEAD = C // HEADS
SLOTS = 26
LANES = 128
TOKENS = 73728
TAIL = WT - LANES
ROWS = WT + 2 * TAIL
GROWS = 3584
STEP = 44
BROWS = 160
LOW = 2
FAR = 4
EPS = 1e-05
F32 = jnp.float32
BF16 = jnp.bfloat16


def dot(a, b):
    return lax.dot_general(a, b, (((1,), (0,)), ((), ())), preferred_element_type=F32)


def dot_nt(a, b):
    return lax.dot_general(a, b, (((1,), (1,)), ((), ())), preferred_element_type=F32)


def dot_tn(a, b):
    return lax.dot_general(a, b, (((0,), (0,)), ((), ())), preferred_element_type=F32)


def norm_stats(widened):
    center = widened - jnp.mean(widened, axis=-1, keepdims=True)
    spread = jnp.mean(center * center, axis=-1, keepdims=True)
    inverse = lax.rsqrt(spread + EPS)
    return center * inverse, inverse


def norm_back(delta_hidden, normal, inverse, gain):
    grad_gain = jnp.sum(delta_hidden * normal, axis=0, keepdims=True)
    delta_normal = delta_hidden * gain
    delta_input = inverse * (
        delta_normal
        - jnp.mean(delta_normal, axis=-1, keepdims=True)
        - normal * jnp.mean(delta_normal * normal, axis=-1, keepdims=True)
    )
    return delta_input, grad_gain


def gather_kernel(table_ref, pos_ref, mask_ref, bias_ref, flat_pos_ref, slots_ref, flat_ref):
    half = WT // 2
    pos = pos_ref[...]
    pos = jnp.concatenate((pos[half:], pos[:half]), axis=0)
    pos = jnp.concatenate((pos[:, half:], pos[:, :half]), axis=1)
    turned = pos[:, LANES:].T
    flat_pos_ref[:WT] = pos[:, :LANES]
    flat_pos_ref[WT : WT + TAIL] = turned[:, :LANES]
    flat_pos_ref[WT + TAIL :] = jnp.zeros((TAIL, LANES), jnp.int32)
    flat_pos_ref[WT + TAIL :, :TAIL] = turned[:, LANES:]
    for h in range(HEADS):
        for g in range(SLOTS):
            count = min(LANES, NPOS - g * LANES)
            row = table_ref[h, :, g * LANES : g * LANES + count]
            slots_ref[h, g, :, :count] = jnp.broadcast_to(row, (8, count))

    def rows(i, carry):
        ats = [pl.ds(pl.multiple_of(i * 16 + 8 * k, 8), 8) for k in range(2)]
        pos = [flat_pos_ref[at, :] for at in ats]
        lane = [jnp.bitwise_and(p, LANES - 1) for p in pos]
        slot = [jnp.right_shift(p, 7) for p in pos]
        held = [[jnp.zeros((8, LANES), F32)] * HEADS for _ in ats]
        for g in range(SLOTS):
            here = [s == g for s in slot]
            for h in range(HEADS):
                row = slots_ref[h, g]
                for k in range(2):
                    got = jnp.take_along_axis(row, lane[k], axis=1)
                    held[k][h] = jnp.where(here[k], got, held[k][h])
        for k, at in enumerate(ats):
            for h in range(HEADS):
                flat_ref[h, at, :] = held[k][h]
        return carry

    lax.fori_loop(0, ROWS // 16, rows, 0)
    mask = jnp.broadcast_to(mask_ref[...], (WT, WT))
    allowed = mask == mask.T
    for h in range(HEADS):
        tail = jnp.concatenate((flat_ref[h, WT : WT + TAIL, :].T, flat_ref[h, WT + TAIL :, :].T[:TAIL]), axis=0)
        at = pl.ds(h * WT, WT)
        bias_ref[at, :LANES] = jnp.where(allowed[:, :LANES], flat_ref[h, :WT, :], -1e30)
        bias_ref[at, LANES:] = jnp.where(allowed[:, LANES:], tail, -1e30)


def bias_pairs(table, pos_index, mask_row):
    return pl.pallas_call(
        gather_kernel,
        out_shape=[jax.ShapeDtypeStruct((HEADS * WT, WT), F32), jax.ShapeDtypeStruct((ROWS, LANES), jnp.int32)],
        scratch_shapes=[pltpu.VMEM((HEADS, SLOTS, 8, LANES), F32), pltpu.VMEM((HEADS, ROWS, LANES), F32)],
        name="bias_pairs",
        compiler_params=pltpu.CompilerParams(vmem_limit_bytes=16 * 1024 * 1024),
        cost_estimate=pl.CostEstimate(flops=10_000_000, bytes_accessed=1_200_000, transcendentals=0),
    )(table, pos_index, mask_row)


def scatter_kernel(pairs_ref, pos_ref, out_ref, sums_ref, packed_ref):
    sums_ref[...] = jnp.zeros_like(sums_ref)
    slot_ids = lax.broadcasted_iota(jnp.int32, (32, LANES), 0)
    lane_ids = lax.broadcasted_iota(jnp.int32, (LANES, LANES), 0)

    def rows(i, carry):
        spread, onehot = [], []
        for j in range(STEP):
            at = pl.ds(i * STEP + j, 1)
            pos = pos_ref[at, :]
            slot = jnp.where(slot_ids == jnp.right_shift(pos, 7), 1.0, 0.0).astype(BF16)
            lane = jnp.bitwise_and(pos, LANES - 1)
            onehot.append(jnp.where(lane_ids == lane, 1.0, 0.0).astype(BF16))
            spread.append(
                jnp.concatenate(
                    [slot * jnp.broadcast_to(pairs_ref[h, at, :], (32, LANES)).astype(BF16) for h in range(HEADS)],
                    axis=0,
                )
            )
        sums_ref[...] += dot_nt(jnp.concatenate(spread, axis=1), jnp.concatenate(onehot, axis=1))
        return carry

    lax.fori_loop(0, ROWS // STEP, rows, 0)
    packed_ref[...] = jnp.zeros_like(packed_ref)
    for h in range(HEADS):
        packed_ref[h * SLOTS : (h + 1) * SLOTS] = sums_ref[h * 32 : h * 32 + SLOTS]
    out_ref[...] = packed_ref[...].astype(BF16)


def bias_grad(pairs, pos_flat):
    return pl.pallas_call(
        scatter_kernel,
        out_shape=jax.ShapeDtypeStruct((BROWS, LANES), BF16),
        scratch_shapes=[pltpu.VMEM((HEADS * 32, LANES), F32), pltpu.VMEM((BROWS, LANES), F32)],
        name="bias_grad",
        compiler_params=pltpu.CompilerParams(vmem_limit_bytes=16 * 1024 * 1024),
        cost_estimate=pl.CostEstimate(flops=1_100_000_000, bytes_accessed=700_000, transcendentals=0),
    )(pairs, pos_flat)


def block_kernel(
    x_ref,
    cot_ref,
    gain_one_ref,
    gain_two_ref,
    qkv_ref,
    proj_ref,
    up_ref,
    down_ref,
    bias_ref,
    out_ref,
    delta_ref,
    grads_out_ref,
    pairs_ref,
    scores_ref,
    prob_ref,
    low_ref,
    grads_ref,
    sems,
):
    factor = HEAD ** (-0.5)
    x = x_ref[...].astype(F32)
    gain_one = gain_one_ref[...]
    gain_two = gain_two_ref[...]
    normal_one, inverse_one = norm_stats(x)
    normed = (normal_one * gain_one).astype(BF16)
    packed = dot(normed, qkv_ref[...]).astype(BF16)
    queries, keys, values = packed[:, :C], packed[:, C : 2 * C], packed[:, 2 * C :]
    head_of = lax.broadcasted_iota(jnp.int32, (WT, C), 1) // HEAD

    def by_head(a):
        return jnp.concatenate([jnp.where(head_of == h, a, jnp.zeros_like(a)) for h in range(HEADS)], axis=0)

    def joined(a):
        out = a[:WT]
        for h in range(1, HEADS):
            out = jnp.where(head_of == h, a[h * WT : (h + 1) * WT], out)
        return out

    queries_by = by_head(queries)
    scores_ref[...] = dot_nt(queries_by, keys)
    for h in range(HEADS):
        at = pl.ds(h * WT, WT)
        scores = scores_ref[at, :] * factor + bias_ref[at, :]
        weight = jnp.exp(scores - jnp.max(scores, axis=-1, keepdims=True))
        prob = weight * (1.0 / jnp.sum(weight, axis=-1, keepdims=True))
        prob_ref[at, :] = prob
        low_ref[at, :] = prob.astype(BF16)
    mixture = joined(dot(low_ref[...], values)).astype(BF16)
    attention = dot(mixture, proj_ref[...]).astype(BF16)

    middle = (x + attention.astype(F32)).astype(BF16)
    widened = middle.astype(F32)
    normal_two, inverse_two = norm_stats(widened)
    normed_two = (normal_two * gain_two).astype(BF16)
    cot = cot_ref[...]
    up_proj = dot(normed_two, up_ref[...])
    cumulative = 0.5 * (1.0 + lax.erf(up_proj * 0.7071067811865476))
    density = jnp.exp(-0.5 * up_proj * up_proj) * 0.3989422804014327
    active = (up_proj * cumulative).astype(BF16)
    out_ref[...] = (widened + dot_nt(active, down_ref[...])).astype(BF16)
    grad_down = dot_tn(cot, active).astype(BF16)
    delta_act = dot(cot, down_ref[...])
    delta_up = (delta_act * (cumulative + up_proj * density)).astype(BF16)
    grad_up = dot_tn(normed_two, delta_up).astype(BF16)
    for t in range(6):
        grads_ref[C * t : C * (t + 1)] = grad_up[:, LANES * t : LANES * (t + 1)]
        grads_ref[C * (t + 6) : C * (t + 7)] = grad_down[:, LANES * t : LANES * (t + 1)]
    cut = C * 12
    early = pltpu.make_async_copy(grads_ref.at[:cut], grads_out_ref.at[:cut], sems.at[0])
    late = pltpu.make_async_copy(grads_ref.at[cut:], grads_out_ref.at[cut:], sems.at[1])
    early.start()
    delta_hidden = dot_nt(delta_up, up_ref[...])
    delta_input, grad_gain_two = norm_back(delta_hidden, normal_two, inverse_two, gain_two)
    delta_middle = (cot.astype(F32) + delta_input).astype(BF16)

    grad_proj = dot_tn(mixture, delta_middle)
    mixture_by = by_head(dot_nt(delta_middle, proj_ref[...]).astype(BF16))
    delta_value = dot_tn(low_ref[...], mixture_by)
    scores_ref[...] = dot_nt(mixture_by, values)
    for h in range(HEADS):
        at = pl.ds(h * WT, WT)
        prob = prob_ref[at, :]
        delta_prob = scores_ref[at, :]
        scores = prob * (delta_prob - jnp.sum(delta_prob * prob, axis=-1, keepdims=True))
        low_ref[at, :] = scores.astype(BF16)
        turned = scores[:, LANES:].T
        pairs_ref[h, :WT, :] = scores[:, :LANES]
        pairs_ref[h, WT : WT + TAIL, :] = turned[:, :LANES]
        pairs_ref[h, WT + TAIL :, :] = jnp.zeros((TAIL, LANES), F32)
        pairs_ref[h, WT + TAIL :, :TAIL] = turned[:, LANES:]
    delta_query = joined(dot(low_ref[...], keys)) * factor
    delta_key = dot_tn(low_ref[...], queries_by) * factor
    delta_packed = jnp.concatenate((delta_query, delta_key, delta_value), axis=1).astype(BF16)
    delta_normed = dot_nt(delta_packed, qkv_ref[...])
    grad_qkv = dot_tn(normed, delta_packed)
    for t in range(4):
        grads_ref[C * (t + 12) : C * (t + 13)] = grad_qkv[:, LANES * t : LANES * (t + 1)].astype(BF16)
    grads_ref[C * 16 : C * 17] = grad_proj[:, :LANES].astype(BF16)
    grads_ref[C * 17 : C * 18] = jnp.concatenate((grad_qkv[:, 4 * LANES :], grad_proj[:, LANES:]), axis=1).astype(BF16)
    delta_normed = delta_normed.astype(BF16).astype(F32)
    delta_input, grad_gain_one = norm_back(delta_normed, normal_one, inverse_one, gain_one)
    delta_ref[...] = (delta_middle.astype(F32) + delta_input).astype(BF16)
    gains = jnp.concatenate((grad_gain_one, grad_gain_two), axis=0)
    wide = jnp.concatenate((gains, jnp.zeros((2, 2 * LANES - C), F32)), axis=1)
    grads_ref[C * 18 :] = jnp.concatenate(
        (wide[:, :LANES], wide[:, LANES:], jnp.zeros((124, LANES), F32)), axis=0
    ).astype(BF16)
    late.start()
    early.wait()
    late.wait()


def block(*args):
    shapes = [
        ((WT, C), BF16),
        ((WT, C), BF16),
        ((GROWS, LANES), BF16),
        ((HEADS, ROWS, LANES), F32),
    ]
    return pl.pallas_call(
        block_kernel,
        out_shape=[jax.ShapeDtypeStruct(s, d) for s, d in shapes],
        scratch_shapes=[
            pltpu.VMEM((HEADS * WT, WT), F32),
            pltpu.VMEM((HEADS * WT, WT), F32),
            pltpu.VMEM((HEADS * WT, WT), BF16),
            pltpu.VMEM((GROWS, LANES), BF16),
            pltpu.SemaphoreType.DMA((2,)),
        ],
        out_specs=[pl.BlockSpec(memory_space=pl.ANY if k == 2 else pltpu.VMEM) for k in range(4)],
        name="block",
        compiler_params=pltpu.CompilerParams(vmem_limit_bytes=24 * 1024 * 1024),
        cost_estimate=pl.CostEstimate(flops=900_000_000, bytes_accessed=4_000_000, transcendentals=300_000),
    )(*args)


def unpack_kernel(
    grads_ref, kept_ref, given_ref, gain_one_ref, gain_two_ref, qkv_ref, proj_ref, up_ref, down_ref, bias_ref
):
    factor = TOKENS ** (-0.5)

    def rows(start, count):
        return grads_ref[start : start + count].astype(F32) * factor

    for t in range(6):
        at = slice(LANES * t, LANES * (t + 1))
        up_ref[:, at] = rows(C * t, C)
        down_ref[:, at] = rows(C * (t + 6), C)
        if t < 4:
            qkv_ref[:, at] = rows(C * (t + 12), C)
    halves = rows(C * 17, C)
    qkv_ref[:, 4 * LANES :] = halves[:, :64]
    proj_ref[:, :LANES] = rows(C * 16, C)
    proj_ref[:, LANES:] = halves[:, 64:]
    gains = rows(C * 18, 16)
    for k, ref in enumerate((gain_one_ref, gain_two_ref)):
        ref[...] = jnp.concatenate((gains[k : k + 1], gains[k + 2 : k + 3, : C - LANES]), axis=1)
    first = lax.axis_index("lon") // FAR % LOW == 0
    kept, given = kept_ref[...].astype(F32), given_ref[...].astype(F32)
    sums = (jnp.where(first, kept, given), jnp.where(first, given, kept))
    for h in range(HEADS):
        for g in range(SLOTS):
            half, row = divmod(h * SLOTS + g, BROWS // LOW)
            count = min(LANES, NPOS - g * LANES)
            bias_ref[h, :, g * LANES : g * LANES + count] = sums[half][row : row + 1, :count]


def unpack(grads, kept, given):
    shapes = [(1, C), (1, C), (C, 3 * C), (C, C), (C, HID), (C, HID), (HEADS, 1, NPOS)]
    return pl.pallas_call(
        unpack_kernel,
        out_shape=[jax.ShapeDtypeStruct(s, F32) for s in shapes],
        name="unpack",
        compiler_params=pltpu.CompilerParams(vmem_limit_bytes=16 * 1024 * 1024),
        cost_estimate=pl.CostEstimate(flops=500_000, bytes_accessed=2_700_000, transcendentals=0),
    )(grads, kept, given)


def neighbours(by):
    lat, lon = lax.axis_size("lat"), lax.axis_size("lon")
    return [
        (i * lon + j, (i + by) % lat * lon + (j + by) % lon) for i in range(lat) for j in range(lon)
    ]


def ring(axis, by):
    peers = lax.axis_size(axis)
    return [(i, (i + by) % peers) for i in range(peers)]


def shift_in(grid):
    def moved(piece, axis, pairs):
        return lax.ppermute(piece.reshape(-1, C), axis, pairs).reshape(piece.shape)

    from_lat = moved(grid[:, :, :3, 6:], "lat", ring("lat", -1))
    from_lon = moved(grid[:, :, 3:, :6], "lon", ring("lon", -1))
    from_both = moved(grid[:, :, :3, :6], ("lat", "lon"), neighbours(-1))
    top = jnp.concatenate((grid[:, :, 3:, 6:], from_lon), axis=3)
    low = jnp.concatenate((from_lat, from_both), axis=3)
    return jnp.concatenate((top, low), axis=2)


def flat_permute(piece, axis):
    return lax.ppermute(piece.reshape(-1, C), axis, ring(axis, 1)).reshape(piece.shape)


def spread_over(axis, groups=None):
    return lambda parts: lax.all_to_all(parts, axis, 0, 0, axis_index_groups=groups)


def total(parts):
    return jnp.sum(parts.astype(F32), axis=0).astype(BF16)


def finish(grid, grads, pairs, pos_flat):
    lat, lon = lax.axis_size("lat"), lax.axis_size("lon")
    low, far = LOW, FAR
    high = lon // (low * far)
    place = lambda h, l, f: (h * low + l) * far + f
    over_low = spread_over(
        ("lat", "lon"),
        [[i * lon + place(h, l, f) for i in range(lat) for l in range(low)] for h in range(high) for f in range(far)],
    )
    over_high = spread_over("lon", [[place(h, l, f) for h in range(high)] for l in range(low) for f in range(far)])
    over_far = spread_over("lon", [[place(h, l, f) for f in range(far)] for h in range(high) for l in range(low)])
    other = [(j, j ^ far) for j in range(lon)]

    def same(part, count):
        return jnp.broadcast_to(part[None], (count,) + part.shape)

    share = GROWS // (lat * low)
    mine = total(over_low(grads.reshape(lat * low, share, LANES)))
    own = bias_grad(pairs, pos_flat).reshape(low, BROWS // low, LANES)
    at = lax.axis_index("lon") // far % low
    kept = lax.dynamic_index_in_dim(own, at, 0, keepdims=False)
    given = lax.dynamic_index_in_dim(own, 1 - at, 0, keepdims=False)
    bias = total(jnp.stack((kept, lax.ppermute(given, "lon", other))))
    both = jnp.concatenate((mine, bias), axis=0)
    rows_got = flat_permute(grid[:, :, 3:], "lat")
    both, rows_got = lax.optimization_barrier((both, rows_got))
    grid = jnp.concatenate((rows_got, grid[:, :, :3]), axis=2)
    cols_got = flat_permute(grid[:, :, :, 6:], "lon")
    both = total(over_high(same(both, high)))
    both, cols_got = lax.optimization_barrier((both, cols_got))
    both = total(over_far(same(both, far)))
    grid = jnp.concatenate((cols_got, grid[:, :, :, :6]), axis=3)
    grads = over_low(same(both[:share], lat * low)).reshape(GROWS, LANES)
    kept = both[share:]
    given = lax.ppermute(kept, "lon", other)
    return grid, grads, kept, given


def local(
    tokens,
    gain_one,
    gain_two,
    qkv_weight,
    proj_weight,
    up_weight,
    down_weight,
    bias_table,
    pos_index,
    mask_ids,
    cotangent,
):
    grid = tokens.shape
    moved = shift_in(jnp.stack((tokens, cotangent)))
    bias, pos_flat = bias_pairs(bias_table.reshape(HEADS, 1, NPOS), pos_index, mask_ids[::-1].reshape(1, WT))
    out, delta, grads, pairs = block(
        moved[0].reshape(WT, C),
        moved[1].reshape(WT, C),
        gain_one.reshape(1, C),
        gain_two.reshape(1, C),
        qkv_weight,
        proj_weight,
        up_weight,
        down_weight.T,
        bias,
    )
    back, grads, kept, given = finish(jnp.stack((out, delta)).reshape((2,) + grid), grads, pairs, pos_flat)
    totals = unpack(grads, kept, given)
    return (
        back[0],
        back[1],
        totals[0].reshape(C),
        totals[1].reshape(C),
        *totals[2:5],
        totals[5].T,
        totals[6].reshape(HEADS, 1, 1, NPOS),
    )


def solution(mesh):
    in_specs = (
        P(None, "lat", "lon", None),
        P(),
        P(),
        P(),
        P(),
        P(),
        P(),
        P(None, None, "lat", None),
        P(),
        P(None, "lat", "lon"),
        P(None, "lat", "lon", None),
    )
    out_specs = (
        P(None, "lat", "lon", None),
        P(None, "lat", "lon", None),
        P(),
        P(),
        P(),
        P(),
        P(),
        P(),
        P(None, None, "lat", None),
    )
    return jax.shard_map(local, mesh=mesh, in_specs=in_specs, out_specs=out_specs, check_vma=False)
```

```python
import jax
import jax.numpy as jnp
from jax import lax
from jax.experimental import pallas as pl
from jax.experimental.pallas import tpu as pltpu
from jax.sharding import PartitionSpec as P

HEADS = 6
WT = 144
NPOS = 3312
C = 192
HID = 768
HEAD = C // HEADS
SLOTS = 26
LANES = 128
TOKENS = 73728
TAIL = WT - LANES
ROWS = WT + 2 * TAIL
GROWS = 3584
STEP = 88
BROWS = 160
LOW = 2
FAR = 4
EPS = 1e-05
F32 = jnp.float32
BF16 = jnp.bfloat16


def dot(a, b):
    return lax.dot_general(a, b, (((1,), (0,)), ((), ())), preferred_element_type=F32)


def dot_nt(a, b):
    return lax.dot_general(a, b, (((1,), (1,)), ((), ())), preferred_element_type=F32)


def dot_tn(a, b):
    return lax.dot_general(a, b, (((0,), (0,)), ((), ())), preferred_element_type=F32)


def norm_stats(widened):
    center = widened - jnp.mean(widened, axis=-1, keepdims=True)
    spread = jnp.mean(center * center, axis=-1, keepdims=True)
    inverse = lax.rsqrt(spread + EPS)
    return center * inverse, inverse


def norm_back(delta_hidden, normal, inverse, gain):
    grad_gain = jnp.sum(delta_hidden * normal, axis=0, keepdims=True)
    delta_normal = delta_hidden * gain
    delta_input = inverse * (
        delta_normal
        - jnp.mean(delta_normal, axis=-1, keepdims=True)
        - normal * jnp.mean(delta_normal * normal, axis=-1, keepdims=True)
    )
    return delta_input, grad_gain


def gather_kernel(table_ref, pos_ref, mask_ref, bias_ref, flat_pos_ref, slots_ref, flat_ref):
    half = WT // 2
    pos = pos_ref[...]
    pos = jnp.concatenate((pos[half:], pos[:half]), axis=0)
    pos = jnp.concatenate((pos[:, half:], pos[:, :half]), axis=1)
    turned = pos[:, LANES:].T
    flat_pos_ref[:WT] = pos[:, :LANES]
    flat_pos_ref[WT : WT + TAIL] = turned[:, :LANES]
    flat_pos_ref[WT + TAIL :] = jnp.zeros((TAIL, LANES), jnp.int32)
    flat_pos_ref[WT + TAIL :, :TAIL] = turned[:, LANES:]
    for h in range(HEADS):
        for g in range(SLOTS):
            count = min(LANES, NPOS - g * LANES)
            row = table_ref[h, :, g * LANES : g * LANES + count]
            slots_ref[h, g, :, :count] = jnp.broadcast_to(row, (8, count))

    def rows(i, carry):
        ats = [pl.ds(pl.multiple_of(i * 16 + 8 * k, 8), 8) for k in range(2)]
        pos = [flat_pos_ref[at, :] for at in ats]
        lane = [jnp.bitwise_and(p, LANES - 1) for p in pos]
        slot = [jnp.right_shift(p, 7) for p in pos]
        held = [[jnp.zeros((8, LANES), F32)] * HEADS for _ in ats]
        for g in range(SLOTS):
            here = [s == g for s in slot]
            for h in range(HEADS):
                row = slots_ref[h, g]
                for k in range(2):
                    got = jnp.take_along_axis(row, lane[k], axis=1)
                    held[k][h] = jnp.where(here[k], got, held[k][h])
        for k, at in enumerate(ats):
            for h in range(HEADS):
                flat_ref[h, at, :] = held[k][h]
        return carry

    lax.fori_loop(0, ROWS // 16, rows, 0)
    mask = jnp.broadcast_to(mask_ref[...], (WT, WT))
    allowed = mask == mask.T
    for h in range(HEADS):
        tail = jnp.concatenate((flat_ref[h, WT : WT + TAIL, :].T, flat_ref[h, WT + TAIL :, :].T[:TAIL]), axis=0)
        at = pl.ds(h * WT, WT)
        bias_ref[at, :LANES] = jnp.where(allowed[:, :LANES], flat_ref[h, :WT, :], -1e30)
        bias_ref[at, LANES:] = jnp.where(allowed[:, LANES:], tail, -1e30)


def bias_pairs(table, pos_index, mask_row):
    return pl.pallas_call(
        gather_kernel,
        out_shape=[jax.ShapeDtypeStruct((HEADS * WT, WT), F32), jax.ShapeDtypeStruct((ROWS, LANES), jnp.int32)],
        scratch_shapes=[pltpu.VMEM((HEADS, SLOTS, 8, LANES), F32), pltpu.VMEM((HEADS, ROWS, LANES), F32)],
        name="bias_pairs",
        compiler_params=pltpu.CompilerParams(vmem_limit_bytes=16 * 1024 * 1024),
        cost_estimate=pl.CostEstimate(flops=10_000_000, bytes_accessed=1_200_000, transcendentals=0),
    )(table, pos_index, mask_row)


def scatter_kernel(pairs_ref, pos_ref, out_ref, sums_ref, packed_ref):
    sums_ref[...] = jnp.zeros_like(sums_ref)
    slot_ids = lax.broadcasted_iota(jnp.int32, (32, LANES), 0)
    lane_ids = lax.broadcasted_iota(jnp.int32, (LANES, LANES), 0)

    def rows(i, carry):
        spread, onehot = [], []
        for j in range(STEP):
            at = pl.ds(i * STEP + j, 1)
            pos = pos_ref[at, :]
            slot = jnp.where(slot_ids == jnp.right_shift(pos, 7), 1.0, 0.0).astype(BF16)
            lane = jnp.bitwise_and(pos, LANES - 1)
            onehot.append(jnp.where(lane_ids == lane, 1.0, 0.0).astype(BF16))
            spread.append(
                jnp.concatenate(
                    [slot * jnp.broadcast_to(pairs_ref[h, at, :], (32, LANES)).astype(BF16) for h in range(HEADS)],
                    axis=0,
                )
            )
        sums_ref[...] += dot_nt(jnp.concatenate(spread, axis=1), jnp.concatenate(onehot, axis=1))
        return carry

    lax.fori_loop(0, ROWS // STEP, rows, 0)
    packed_ref[...] = jnp.zeros_like(packed_ref)
    for h in range(HEADS):
        packed_ref[h * SLOTS : (h + 1) * SLOTS] = sums_ref[h * 32 : h * 32 + SLOTS]
    out_ref[...] = packed_ref[...].astype(BF16)


def bias_grad(pairs, pos_flat):
    return pl.pallas_call(
        scatter_kernel,
        out_shape=jax.ShapeDtypeStruct((BROWS, LANES), BF16),
        scratch_shapes=[pltpu.VMEM((HEADS * 32, LANES), F32), pltpu.VMEM((BROWS, LANES), F32)],
        name="bias_grad",
        compiler_params=pltpu.CompilerParams(vmem_limit_bytes=16 * 1024 * 1024),
        cost_estimate=pl.CostEstimate(flops=1_100_000_000, bytes_accessed=700_000, transcendentals=0),
    )(pairs, pos_flat)


def block_kernel(
    x_ref,
    cot_ref,
    gain_one_ref,
    gain_two_ref,
    qkv_ref,
    proj_ref,
    up_ref,
    down_ref,
    bias_ref,
    out_ref,
    delta_ref,
    grads_ref,
    pairs_ref,
    scores_ref,
    prob_ref,
    low_ref,
):
    factor = HEAD ** (-0.5)
    x = x_ref[...].astype(F32)
    gain_one = gain_one_ref[...]
    gain_two = gain_two_ref[...]
    normal_one, inverse_one = norm_stats(x)
    normed = (normal_one * gain_one).astype(BF16)
    packed = dot(normed, qkv_ref[...]).astype(BF16)
    queries, keys, values = packed[:, :C], packed[:, C : 2 * C], packed[:, 2 * C :]
    head_of = lax.broadcasted_iota(jnp.int32, (WT, C), 1) // HEAD

    def by_head(a):
        return jnp.concatenate([jnp.where(head_of == h, a, jnp.zeros_like(a)) for h in range(HEADS)], axis=0)

    def joined(a):
        out = a[:WT]
        for h in range(1, HEADS):
            out = jnp.where(head_of == h, a[h * WT : (h + 1) * WT], out)
        return out

    queries_by = by_head(queries)
    scores_ref[...] = dot_nt(queries_by, keys)
    for h in range(HEADS):
        at = pl.ds(h * WT, WT)
        scores = scores_ref[at, :] * factor + bias_ref[at, :]
        weight = jnp.exp(scores - jnp.max(scores, axis=-1, keepdims=True))
        prob = weight * (1.0 / jnp.sum(weight, axis=-1, keepdims=True))
        prob_ref[at, :] = prob
        low_ref[at, :] = prob.astype(BF16)
    mixture = joined(dot(low_ref[...], values)).astype(BF16)
    attention = dot(mixture, proj_ref[...]).astype(BF16)

    middle = (x + attention.astype(F32)).astype(BF16)
    widened = middle.astype(F32)
    normal_two, inverse_two = norm_stats(widened)
    normed_two = (normal_two * gain_two).astype(BF16)
    cot = cot_ref[...]
    up_proj = dot(normed_two, up_ref[...])
    cumulative = 0.5 * (1.0 + lax.erf(up_proj * 0.7071067811865476))
    density = jnp.exp(-0.5 * up_proj * up_proj) * 0.3989422804014327
    active = (up_proj * cumulative).astype(BF16)
    out_ref[...] = (widened + dot_nt(active, down_ref[...])).astype(BF16)
    grad_down = dot_tn(cot, active).astype(BF16)
    delta_act = dot(cot, down_ref[...])
    delta_up = (delta_act * (cumulative + up_proj * density)).astype(BF16)
    grad_up = dot_tn(normed_two, delta_up).astype(BF16)
    for t in range(6):
        grads_ref[C * t : C * (t + 1)] = grad_up[:, LANES * t : LANES * (t + 1)]
        grads_ref[C * (t + 6) : C * (t + 7)] = grad_down[:, LANES * t : LANES * (t + 1)]
    delta_hidden = dot_nt(delta_up, up_ref[...])
    delta_input, grad_gain_two = norm_back(delta_hidden, normal_two, inverse_two, gain_two)
    delta_middle = (cot.astype(F32) + delta_input).astype(BF16)

    grad_proj = dot_tn(mixture, delta_middle)
    mixture_by = by_head(dot_nt(delta_middle, proj_ref[...]).astype(BF16))
    delta_value = dot_tn(low_ref[...], mixture_by)
    scores_ref[...] = dot_nt(mixture_by, values)
    for h in range(HEADS):
        at = pl.ds(h * WT, WT)
        prob = prob_ref[at, :]
        delta_prob = scores_ref[at, :]
        scores = prob * (delta_prob - jnp.sum(delta_prob * prob, axis=-1, keepdims=True))
        low_ref[at, :] = scores.astype(BF16)
        turned = scores[:, LANES:].T
        pairs_ref[h, :WT, :] = scores[:, :LANES]
        pairs_ref[h, WT : WT + TAIL, :] = turned[:, :LANES]
        pairs_ref[h, WT + TAIL :, :] = jnp.zeros((TAIL, LANES), F32)
        pairs_ref[h, WT + TAIL :, :TAIL] = turned[:, LANES:]
    delta_query = joined(dot(low_ref[...], keys)) * factor
    delta_key = dot_tn(low_ref[...], queries_by) * factor
    delta_packed = jnp.concatenate((delta_query, delta_key, delta_value), axis=1).astype(BF16)
    delta_normed = dot_nt(delta_packed, qkv_ref[...])
    grad_qkv = dot_tn(normed, delta_packed)
    for t in range(4):
        grads_ref[C * (t + 12) : C * (t + 13)] = grad_qkv[:, LANES * t : LANES * (t + 1)].astype(BF16)
    grads_ref[C * 16 : C * 17] = grad_proj[:, :LANES].astype(BF16)
    grads_ref[C * 17 : C * 18] = jnp.concatenate((grad_qkv[:, 4 * LANES :], grad_proj[:, LANES:]), axis=1).astype(BF16)
    delta_normed = delta_normed.astype(BF16).astype(F32)
    delta_input, grad_gain_one = norm_back(delta_normed, normal_one, inverse_one, gain_one)
    delta_ref[...] = (delta_middle.astype(F32) + delta_input).astype(BF16)
    gains = jnp.concatenate((grad_gain_one, grad_gain_two), axis=0)
    wide = jnp.concatenate((gains, jnp.zeros((2, 2 * LANES - C), F32)), axis=1)
    grads_ref[C * 18 :] = jnp.concatenate(
        (wide[:, :LANES], wide[:, LANES:], jnp.zeros((124, LANES), F32)), axis=0
    ).astype(BF16)


def block(*args):
    shapes = [
        ((WT, C), BF16),
        ((WT, C), BF16),
        ((GROWS, LANES), BF16),
        ((HEADS, ROWS, LANES), F32),
    ]
    return pl.pallas_call(
        block_kernel,
        out_shape=[jax.ShapeDtypeStruct(s, d) for s, d in shapes],
        scratch_shapes=[
            pltpu.VMEM((HEADS * WT, WT), F32),
            pltpu.VMEM((HEADS * WT, WT), F32),
            pltpu.VMEM((HEADS * WT, WT), BF16),
        ],
        name="block",
        compiler_params=pltpu.CompilerParams(vmem_limit_bytes=24 * 1024 * 1024),
        cost_estimate=pl.CostEstimate(flops=900_000_000, bytes_accessed=4_000_000, transcendentals=300_000),
    )(*args)


def unpack_kernel(
    grads_ref, kept_ref, given_ref, gain_one_ref, gain_two_ref, qkv_ref, proj_ref, up_ref, down_ref, bias_ref
):
    factor = TOKENS ** (-0.5)

    def rows(start, count):
        return grads_ref[start : start + count].astype(F32) * factor

    for t in range(6):
        at = slice(LANES * t, LANES * (t + 1))
        up_ref[:, at] = rows(C * t, C)
        down_ref[:, at] = rows(C * (t + 6), C)
        if t < 4:
            qkv_ref[:, at] = rows(C * (t + 12), C)
    halves = rows(C * 17, C)
    qkv_ref[:, 4 * LANES :] = halves[:, :64]
    proj_ref[:, :LANES] = rows(C * 16, C)
    proj_ref[:, LANES:] = halves[:, 64:]
    gains = rows(C * 18, 16)
    for k, ref in enumerate((gain_one_ref, gain_two_ref)):
        ref[...] = jnp.concatenate((gains[k : k + 1], gains[k + 2 : k + 3, : C - LANES]), axis=1)
    first = lax.axis_index("lon") // FAR % LOW == 0
    kept, given = kept_ref[...].astype(F32), given_ref[...].astype(F32)
    sums = (jnp.where(first, kept, given), jnp.where(first, given, kept))
    for h in range(HEADS):
        for g in range(SLOTS):
            half, row = divmod(h * SLOTS + g, BROWS // LOW)
            count = min(LANES, NPOS - g * LANES)
            bias_ref[h, :, g * LANES : g * LANES + count] = sums[half][row : row + 1, :count]


def unpack(grads, kept, given):
    shapes = [(1, C), (1, C), (C, 3 * C), (C, C), (C, HID), (C, HID), (HEADS, 1, NPOS)]
    return pl.pallas_call(
        unpack_kernel,
        out_shape=[jax.ShapeDtypeStruct(s, F32) for s in shapes],
        name="unpack",
        compiler_params=pltpu.CompilerParams(vmem_limit_bytes=16 * 1024 * 1024),
        cost_estimate=pl.CostEstimate(flops=500_000, bytes_accessed=2_700_000, transcendentals=0),
    )(grads, kept, given)


def neighbours(by):
    lat, lon = lax.axis_size("lat"), lax.axis_size("lon")
    return [
        (i * lon + j, (i + by) % lat * lon + (j + by) % lon) for i in range(lat) for j in range(lon)
    ]


def ring(axis, by):
    peers = lax.axis_size(axis)
    return [(i, (i + by) % peers) for i in range(peers)]


def shift_in(grid):
    def moved(piece, axis, pairs):
        return lax.ppermute(piece.reshape(-1, C), axis, pairs).reshape(piece.shape)

    from_lat = moved(grid[:, :, :3, 6:], "lat", ring("lat", -1))
    from_lon = moved(grid[:, :, 3:, :6], "lon", ring("lon", -1))
    from_both = moved(grid[:, :, :3, :6], ("lat", "lon"), neighbours(-1))
    top = jnp.concatenate((grid[:, :, 3:, 6:], from_lon), axis=3)
    low = jnp.concatenate((from_lat, from_both), axis=3)
    return jnp.concatenate((top, low), axis=2)


def flat_permute(piece, axis):
    return lax.ppermute(piece.reshape(-1, C), axis, ring(axis, 1)).reshape(piece.shape)


def spread_over(axis, groups=None):
    return lambda parts: lax.all_to_all(parts, axis, 0, 0, axis_index_groups=groups)


def total(parts):
    return jnp.sum(parts.astype(F32), axis=0).astype(BF16)


def finish(grid, grads, pairs, pos_flat):
    lat, lon = lax.axis_size("lat"), lax.axis_size("lon")
    low, far = LOW, FAR
    high = lon // (low * far)
    place = lambda h, l, f: (h * low + l) * far + f
    over_low = spread_over(
        ("lat", "lon"),
        [[i * lon + place(h, l, f) for i in range(lat) for l in range(low)] for h in range(high) for f in range(far)],
    )
    over_high = spread_over("lon", [[place(h, l, f) for h in range(high)] for l in range(low) for f in range(far)])
    over_far = spread_over("lon", [[place(h, l, f) for f in range(far)] for h in range(high) for l in range(low)])
    other = [(j, j ^ far) for j in range(lon)]

    def same(part, count):
        return jnp.broadcast_to(part[None], (count,) + part.shape)

    share = GROWS // (lat * low)
    mine = total(over_low(grads.reshape(lat * low, share, LANES)))
    own = bias_grad(pairs, pos_flat).reshape(low, BROWS // low, LANES)
    at = lax.axis_index("lon") // far % low
    kept = lax.dynamic_index_in_dim(own, at, 0, keepdims=False)
    given = lax.dynamic_index_in_dim(own, 1 - at, 0, keepdims=False)
    bias = total(jnp.stack((kept, lax.ppermute(given, "lon", other))))
    both = jnp.concatenate((mine, bias), axis=0)
    rows_got = flat_permute(grid[:, :, 3:], "lat")
    both, rows_got = lax.optimization_barrier((both, rows_got))
    grid = jnp.concatenate((rows_got, grid[:, :, :3]), axis=2)
    cols_got = flat_permute(grid[:, :, :, 6:], "lon")
    both = total(over_high(same(both, high)))
    both, cols_got = lax.optimization_barrier((both, cols_got))
    both = total(over_far(same(both, far)))
    grid = jnp.concatenate((cols_got, grid[:, :, :, :6]), axis=3)
    grads = over_low(same(both[:share], lat * low)).reshape(GROWS, LANES)
    kept = both[share:]
    given = lax.ppermute(kept, "lon", other)
    return grid, grads, kept, given


def local(
    tokens,
    gain_one,
    gain_two,
    qkv_weight,
    proj_weight,
    up_weight,
    down_weight,
    bias_table,
    pos_index,
    mask_ids,
    cotangent,
):
    grid = tokens.shape
    moved = shift_in(jnp.stack((tokens, cotangent)))
    bias, pos_flat = bias_pairs(bias_table.reshape(HEADS, 1, NPOS), pos_index, mask_ids[::-1].reshape(1, WT))
    out, delta, grads, pairs = block(
        moved[0].reshape(WT, C),
        moved[1].reshape(WT, C),
        gain_one.reshape(1, C),
        gain_two.reshape(1, C),
        qkv_weight,
        proj_weight,
        up_weight,
        down_weight.T,
        bias,
    )
    back, grads, kept, given = finish(jnp.stack((out, delta)).reshape((2,) + grid), grads, pairs, pos_flat)
    totals = unpack(grads, kept, given)
    return (
        back[0],
        back[1],
        totals[0].reshape(C),
        totals[1].reshape(C),
        *totals[2:5],
        totals[5].T,
        totals[6].reshape(HEADS, 1, 1, NPOS),
    )


def solution(mesh):
    in_specs = (
        P(None, "lat", "lon", None),
        P(),
        P(),
        P(),
        P(),
        P(),
        P(),
        P(None, None, "lat", None),
        P(),
        P(None, "lat", "lon"),
        P(None, "lat", "lon", None),
    )
    out_specs = (
        P(None, "lat", "lon", None),
        P(None, "lat", "lon", None),
        P(),
        P(),
        P(),
        P(),
        P(),
        P(),
        P(None, None, "lat", None),
    )
    return jax.shard_map(local, mesh=mesh, in_specs=in_specs, out_specs=out_specs, check_vma=False)
```
